128 devices in a mesh: row: 8 (over x, z_hi), col: 16 (over y, z_lo, core).
Axes of the slice: x: 4, y: 4, z: 4 (z_hi: 2, z_lo: 2; z = z_hi * 2 + z_lo), core: 2. Of those that a mesh axis runs over, the one named last changes fastest.
Arguments:
- tokens: bfloat16 [128, 1024, 256], P('row', 'col'), may hold values from -6 to 6
- grad_out: bfloat16 [128, 1024, 256], P('row', 'col'), may hold values from -6 to 6
- scales: float32 [2, 256], replicated, may hold values from 0.1 to 1.9
- w_qkv: bfloat16 [256, 768], replicated
- w_out: bfloat16 [256, 256], replicated, may hold values from -0.375 to 0.375
- w_up: bfloat16 [256, 768], replicated, may hold values from -0.375 to 0.375
- w_down: bfloat16 [768, 256], replicated, may hold values from -0.21875 to 0.21875
Outputs:
- grad_tokens: bfloat16 [128, 1024, 256], P('row', 'col')
- grad_qkv: float32 [256, 768], P(('row', 'col'))
- grad_wout: float32 [256, 256], P(('row', 'col'))
- grad_up: float32 [256, 768], P(('row', 'col'))
- grad_down: float32 [768, 256], P(('row', 'col'))
- grad_scales: float32 [2, 256], replicated
The draws below stay inside these ranges and needn't reach their ends.
All inputs are finite; a program needn't handle non-finite values.
Results may differ from the reference program's by a relative error of at most 0.015.
Values may be sent and summed in bfloat16 or wider, within the bound.
No kernel may reach another device: no remote copies, remote signals or barrier semaphores. Data moves between devices by JAX's collectives and lax.ppermute only.
A program may use at most 128 MiB of HBM per device.

```python
import math
from functools import partial
import jax
import jax.numpy as jnp
from jax import lax

C = 256
HEADS = 4
FF = 768
NY = 128
NX = 1024
TOKENS = 131072


def draw_w_qkv(key, part):
    key = jax.random.fold_in(key, 11)
    first = jax.random.fold_in(key, 0)
    whole = jax.random.normal(first, (C, 3 * C), jnp.float32) / math.sqrt(C)
    return whole.astype(jnp.bfloat16)


def level_of(key, extent, cuts, low, top_value):
    level = 1.0
    for axis_at, blocks in cuts:
        heights = jax.random.uniform(jax.random.fold_in(jax.random.fold_in(key, 6), axis_at), (blocks,), jnp.float32, low / len(cuts), top_value / len(cuts))
        level = level * jnp.repeat(jnp.exp(heights), extent[axis_at] // blocks).reshape((-1,) + (1,) * (len(extent) - 1 - axis_at))
    return level


def bell_draw(stream_key, dims, deviation, bound, shards=(), kind=jnp.bfloat16):
    loudness = level_of(stream_key, dims, shards, -0.22, 0.18) if shards else 1.0
    drawn = jax.random.normal(stream_key, dims, jnp.float32) * deviation * loudness
    return jnp.minimum(jnp.maximum(drawn, -bound), bound).astype(kind)


def setup_inputs(seed: int = 0) -> dict:
    seeds = jax.random.split(jax.random.key(seed), 8)
    tokens = bell_draw(seeds[0], (NY, NX, C), 1.0, 6.0, ((0, 8), (1, 16)))
    grad_out = bell_draw(seeds[1], (NY, NX, C), 1.0, 6.0, ((0, 8), (1, 16)))
    scales = jnp.clip(1.0 + 0.18 * jax.random.normal(seeds[2], (2, C), jnp.float32), 0.1, 1.9)
    w_qkv = draw_w_qkv(jax.random.fold_in(seeds[7], 71), 0)
    w_out = bell_draw(seeds[4], (C, C), C ** -0.5, 0.375)
    w_up = bell_draw(seeds[5], (C, FF), C ** -0.5, 0.375)
    w_down = bell_draw(seeds[6], (FF, C), FF ** -0.5, 0.21875)
    return dict(tokens=tokens, grad_out=grad_out, scales=scales, w_qkv=w_qkv, w_out=w_out, w_up=w_up, w_down=w_down)


def norm_parts(values):
    inverse = lax.rsqrt(lax.optimization_barrier(jnp.mean(values * values, axis=-1, keepdims=True)) + 1e-06)
    return (values * inverse, inverse)

def norm_back(grad_h, gain, normed, inverse):
    grad_n = grad_h * gain
    grad_x = inverse * (grad_n - normed * lax.optimization_barrier(jnp.mean(grad_n * normed, axis=-1, keepdims=True)))
    return (grad_x, lax.optimization_barrier(jnp.sum(grad_h * normed, axis=(0, 1))))

def window_start(position, total):
    return jnp.clip(position - 3, 0, total - 7)

def window_index(row_start):
    query_rows = row_start + jnp.arange(4, dtype=jnp.int32)
    row_index = window_start(query_rows, NY)[:, None] + jnp.arange(7, dtype=jnp.int32)[None, :] - row_start + 6
    query_cols = jnp.arange(NX, dtype=jnp.int32)
    col_index = window_start(query_cols, NX)[:, None] + jnp.arange(7, dtype=jnp.int32)[None, :] + 6
    return (row_index.astype(jnp.int32), col_index.astype(jnp.int32))

def window_gather(key_slab, row_index, col_index):
    picked = jnp.take(key_slab, row_index, axis=0)
    picked = jnp.take(picked, col_index, axis=2)
    picked = jnp.transpose(picked, (0, 2, 1, 3, 4))
    return picked.reshape(4, NX, 49, key_slab.shape[-1])

def block_softmax(queries, padded, index):
    head_dim = C // HEADS
    factor = 1.0 / math.sqrt(head_dim)
    row_start = (index * 4).astype(jnp.int32)
    zero = jnp.zeros((), jnp.int32)
    query_blk = lax.dynamic_slice(queries, (row_start, zero, zero), (4, NX, C))
    key_slab = lax.dynamic_slice(padded, (row_start, zero, zero), (16, NX + 12, 2 * C))
    row_index, col_index = window_index(row_start)
    window = window_gather(key_slab, row_index, col_index)
    key_win = window[..., :C].astype(jnp.float32).reshape(4, NX, 49, HEADS, head_dim)
    value_win = window[..., C:].astype(jnp.float32).reshape(4, NX, 49, HEADS, head_dim)
    query_f = query_blk.astype(jnp.float32).reshape(4, NX, HEADS, head_dim)
    scores = jnp.einsum('inhd,inkhd->inhk', query_f, key_win) * factor
    top = lax.optimization_barrier(jnp.max(scores, axis=-1, keepdims=True))
    expon = jnp.exp(scores - top)
    weights_soft = expon / lax.optimization_barrier(jnp.sum(expon, axis=-1, keepdims=True))
    rounded = lax.optimization_barrier(weights_soft.astype(jnp.bfloat16)).astype(jnp.float32)
    return (query_f, key_win, value_win, weights_soft, rounded, row_index, col_index, row_start)

def reference(tokens, grad_out, scales, w_qkv, w_out, w_up, w_down):
    head_dim = C // HEADS
    factor = 1.0 / math.sqrt(head_dim)
    flat = NY * NX
    tokens_f = tokens.astype(jnp.float32)
    normed1, inverse1 = norm_parts(tokens_f)
    hidden1 = (normed1 * scales[0]).astype(jnp.bfloat16)
    projected = jnp.dot(hidden1.reshape(flat, C), w_qkv, preferred_element_type=jnp.float32).astype(jnp.bfloat16)
    projected = projected.reshape(NY, NX, 3 * C)
    queries = projected[..., :C]
    padded = jnp.pad(projected[..., C:], ((6, 6), (6, 6), (0, 0)))
    blocks = jnp.arange(NY // 4, dtype=jnp.int32)

    def forward_block(index):
        parts = block_softmax(queries, padded, index)
        out = jnp.einsum('inhk,inkhd->inhd', parts[4], parts[2])
        return out.reshape(4, NX, C).astype(jnp.bfloat16)
    attended = lax.map(forward_block, blocks).reshape(NY, NX, C)
    mixed = jnp.dot(attended.reshape(flat, C), w_out, preferred_element_type=jnp.float32).reshape(NY, NX, C)
    resid = (tokens_f + mixed).astype(jnp.bfloat16)
    normed2, inverse2 = norm_parts(resid.astype(jnp.float32))
    hidden2 = (normed2 * scales[1]).astype(jnp.bfloat16).reshape(flat, C)
    pre_act = jnp.dot(hidden2, w_up, preferred_element_type=jnp.float32)
    activ, gelu_back = jax.vjp(partial(jax.nn.gelu, approximate=True), pre_act)
    activ = activ.astype(jnp.bfloat16)
    grad_flat = grad_out.reshape(flat, C)
    g_down = jnp.dot(activ.T, grad_flat, preferred_element_type=jnp.float32)
    grad_act = jnp.dot(grad_flat, w_down.T, preferred_element_type=jnp.float32)
    grad_pre = gelu_back(grad_act)[0].astype(jnp.bfloat16)
    g_up = jnp.dot(hidden2.T, grad_pre, preferred_element_type=jnp.float32)
    grad_h2 = jnp.dot(grad_pre, w_up.T, preferred_element_type=jnp.float32).reshape(NY, NX, C)
    back2, g_scale2 = norm_back(grad_h2, scales[1], normed2, inverse2)
    grad_resid = (grad_out.astype(jnp.float32) + back2).astype(jnp.bfloat16)
    resid_flat = grad_resid.reshape(flat, C)
    g_out = jnp.dot(attended.reshape(flat, C).T, resid_flat, preferred_element_type=jnp.float32)
    grad_att = jnp.dot(resid_flat, w_out.T, preferred_element_type=jnp.float32).astype(jnp.bfloat16).reshape(NY, NX, C)

    def backward_block(accum, index):
        query_f, key_win, value_win, weights_soft, rounded, row_index, col_index, row_start = block_softmax(queries, padded, index)
        zero = jnp.zeros((), jnp.int32)
        grad_blk = lax.dynamic_slice(grad_att, (row_start, zero, zero), (4, NX, C)).astype(jnp.float32).reshape(4, NX, HEADS, head_dim)
        out_blk = lax.dynamic_slice(attended, (row_start, zero, zero), (4, NX, C)).astype(jnp.float32).reshape(4, NX, HEADS, head_dim)
        grad_soft = jnp.einsum('inhd,inkhd->inhk', grad_blk, value_win)
        inner = lax.optimization_barrier(jnp.sum(grad_blk * out_blk, axis=-1))[..., None]
        grad_scores = lax.optimization_barrier((weights_soft * (grad_soft - inner)).astype(jnp.bfloat16)).astype(jnp.float32)
        grad_query = (jnp.einsum('inhk,inkhd->inhd', grad_scores, key_win) * factor).reshape(4, NX, C).astype(jnp.bfloat16)
        grad_keys = (jnp.einsum('inhk,inhd->inkhd', grad_scores, query_f) * factor).reshape(4, NX, 49, C)
        grad_vals = jnp.einsum('inhk,inhd->inkhd', rounded, grad_blk).reshape(4, NX, 49, C)
        rows_at = jnp.broadcast_to(row_index[:, None, :, None], (4, NX, 7, 7)).reshape(4, NX, 49)
        cols_at = jnp.broadcast_to(col_index[None, :, None, :], (4, NX, 7, 7)).reshape(4, NX, 49)
        key_part = jnp.zeros((16, NX + 12, C), jnp.float32).at[rows_at, cols_at].add(grad_keys)
        value_part = jnp.zeros((16, NX + 12, C), jnp.float32).at[rows_at, cols_at].add(grad_vals)
        grad_slab = jnp.concatenate((key_part, value_part), axis=-1)
        current = lax.dynamic_slice(accum, (row_start, zero, zero), (16, NX + 12, 2 * C))
        accum = lax.dynamic_update_slice(accum, current + grad_slab, (row_start, zero, zero))
        return (accum, grad_query)
    accum0 = jnp.zeros((NY + 12, NX + 12, 2 * C), jnp.float32)
    accum, grad_q_blocks = lax.scan(backward_block, accum0, blocks)
    grad_q = grad_q_blocks.reshape(NY, NX, C)
    grad_kv = accum[6:NY + 6, 6:NX + 6].astype(jnp.bfloat16)
    grad_proj = jnp.concatenate((grad_q, grad_kv), axis=-1).reshape(flat, 3 * C)
    g_qkv = jnp.dot(hidden1.reshape(flat, C).T, grad_proj, preferred_element_type=jnp.float32)
    grad_h1 = jnp.dot(grad_proj, w_qkv.T, preferred_element_type=jnp.float32).reshape(NY, NX, C)
    back1, g_scale1 = norm_back(grad_h1, scales[0], normed1, inverse1)
    grad_tokens = (grad_resid.astype(jnp.float32) + back1).astype(jnp.bfloat16)
    loss_scale = 1.0 / math.sqrt(TOKENS)
    g_scales = jnp.stack((g_scale1, g_scale2)) * loss_scale
    return (grad_tokens, g_qkv * loss_scale, g_out * loss_scale, g_up * loss_scale, g_down * loss_scale, g_scales)
```

```python
import functools
import math

import jax
import jax.numpy as jnp
from jax import lax
from jax.experimental import pallas as pl
from jax.experimental.pallas import tpu as pltpu
from jax.sharding import Mesh, PartitionSpec as P

HEADS = 4
C = 256
FF = 768
TR, TC = 16, 64
ER, EC = 22, 80
KR, KC = 14, 16
NK = KR * KC
NB = 16
CHUNK = 48
EPS = 1e-6
NEG = -1e30
BF = jnp.bfloat16
F32 = jnp.float32
GA = math.sqrt(2.0 / math.pi)
GB = GA * 0.044715

ROW = ("x", "zh")
COL = ("y", "zl", "core")
CHIPS = ("x", "zh", "y", "zl")


def nt(a, b):
    return lax.dot_general(a, b, (((1,), (1,)), ((), ())), preferred_element_type=F32)


def tn(a, b):
    return lax.dot_general(a, b, (((0,), (0,)), ((), ())), preferred_element_type=F32)


def nn(a, b):
    return jnp.dot(a, b, preferred_element_type=F32)


def norm(x):
    inverse = lax.rsqrt(jnp.mean(x * x, axis=-1, keepdims=True) + EPS)
    return x * inverse, inverse


def head_masks():
    lane = lax.broadcasted_iota(jnp.int32, (1, C), 1)
    return [(jnp.right_shift(lane, 6) == h).astype(F32) for h in range(HEADS)]


def expand(x, masks):
    return jnp.concatenate([x * m for m in masks], axis=0).astype(BF)


def pick(x, masks):
    out = x[0:64] * masks[0]
    for h in range(1, HEADS):
        out = out + x[64 * h : 64 * h + 64] * masks[h]
    return out


def main_kernel(
    pos,
    tok_ext,
    tok,
    gout,
    scales,
    w_qkv,
    w_out,
    w_up,
    w_down,
    o_gr,
    o_dq,
    o_core,
    o_left,
    o_right,
    o_top,
    o_bottom,
    o_keep,
    o_send,
    bias,
    kv,
    dkv,
    q,
    att,
    gatt,
    dq,
    probs,
    h1e,
    h1l,
    attb,
    h2,
    activ,
    gpre,
    gmat,
    gdown,
    pk,
    side,
    gsc2,
    *,
    rows_total,
    cols_total,
):
    base_r, base_c, core = pos[0], pos[1], pos[2]
    masks = head_masks()

    key = lax.broadcasted_iota(jnp.int32, (NK, 1), 0)
    lane = jnp.bitwise_and(lax.broadcasted_iota(jnp.int32, (1, 256), 1), 63)
    for rb in range(2):
        k_row = base_r + rb * 8 - 3 + jnp.right_shift(key, 4)
        q_row = base_r + rb * 8 + jnp.right_shift(lane, 3)
        s_row = jnp.clip(q_row - 3, 0, rows_total - 7)
        row_ok = (k_row >= s_row) & (k_row <= s_row + 6)
        for kind, c0 in enumerate((0, 8, 56)):
            k_col = base_c + c0 - 3 + jnp.bitwise_and(key, 15)
            q_col = base_c + c0 + jnp.bitwise_and(lane, 7)
            s_col = jnp.clip(q_col - 3, 0, cols_total - 7)
            ok = row_ok & (k_col >= s_col) & (k_col <= s_col + 6)
            bias[rb * 3 + kind] = jnp.where(ok, 0.0, NEG)

    s0 = scales[0:1, :]
    s1 = scales[1:2, :]

    def project(i, carry):
        x = tok_ext[pl.ds(i * 2, 2)].reshape(2 * EC, C).astype(F32)
        h = (norm(x)[0] * s0).astype(BF)
        h1e[pl.ds(pl.multiple_of(i * 2 * EC, 16), 2 * EC), :] = h
        kv[pl.ds(i * 2, 2)] = nn(h, w_qkv[:, C:]).reshape(2, EC, 2 * C)
        dkv[pl.ds(i * 2, 2)] = jnp.zeros((2, EC, 2 * C), F32)
        return carry

    lax.fori_loop(0, ER // 2, project, 0)

    def project_q(i, carry):
        at = pl.ds(pl.multiple_of(i * 256, 256), 256)
        h = (norm(tok[at, :].astype(F32))[0] * s0).astype(BF)
        h1l[at, :] = h
        got = nn(h, w_qkv[:, :C]).astype(BF).astype(F32) * 0.125
        q[pl.ds(i * 4, 4)] = got.reshape(4, TC, C)
        return carry

    lax.fori_loop(0, 4, project_q, 0)

    def place(i):
        rb = jnp.right_shift(i, 3)
        cb = jnp.bitwise_and(i, 7)
        return rb, cb, pl.multiple_of(rb * 8, 8), pl.multiple_of(cb * 8, 8)

    def block_of(ref, r0, c0):
        return ref[pl.ds(r0, 8), pl.ds(c0, 8), :].reshape(64, C)

    def slab_of(r0, c0):
        return kv[pl.ds(r0, KR), pl.ds(c0, KC), :].astype(BF).reshape(NK, 2 * C)

    def forward(i, carry):
        rb, cb, r0, c0 = place(i)
        slab = slab_of(r0, c0)
        qe = expand(block_of(q, r0, c0), masks)
        kind = jnp.where(cb == 0, 0, jnp.where(cb == 7, 2, 1))
        s = nt(slab[:, :C], qe) + bias[rb * 3 + kind]
        e = jnp.exp(s - jnp.max(s, axis=0, keepdims=True))
        p = (e * (1.0 / jnp.sum(e, axis=0, keepdims=True))).astype(BF)
        probs[i] = p
        out = pick(tn(p, slab[:, C:]), masks)
        att[pl.ds(r0, 8), pl.ds(c0, 8), :] = out.reshape(8, 8, C)
        return carry

    lax.fori_loop(0, NB, forward, 0)

    gsc2[...] = jnp.zeros_like(gsc2)

    def feed(i, carry):
        at = pl.ds(pl.multiple_of(i * 256, 256), 256)
        a = att[pl.ds(i * 4, 4)].reshape(256, C).astype(BF)
        attb[at, :] = a
        resid = (tok[at, :].astype(F32) + nn(a, w_out[...])).astype(BF).astype(F32)
        n2, inv2 = norm(resid)
        h = (n2 * s1).astype(BF)
        h2[at, :] = h
        x = nn(h, w_up[...])
        g = gout[at, :]
        ga = nt(g, w_down[...])
        xx = x * x
        t = jnp.tanh(x * (GA + GB * xx))
        half = 0.5 + 0.5 * t
        act = x * half
        activ[at, :] = act.astype(BF)
        gp = (ga * (half + act * (1.0 - t) * (GA + (3.0 * GB) * xx))).astype(BF)
        gpre[at, :] = gp
        gh = nt(gp, w_up[...])
        gn = gh * s1
        back = inv2 * (gn - n2 * jnp.mean(gn * n2, axis=-1, keepdims=True))
        gsc2[...] += jnp.sum(gh * n2, axis=0, keepdims=True)
        gr = (g.astype(F32) + back).astype(BF)
        o_gr[at, :] = gr
        gatt[pl.ds(i * 4, 4)] = nt(gr, w_out[...]).astype(BF).astype(F32).reshape(4, TC, C)
        return carry

    lax.fori_loop(0, 4, feed, 0)

    def put(first, value):
        for n in range(value.shape[1] // 128):
            gmat[first + n] = value[:, n * 128 : n * 128 + 128]

    put(6, tn(attb[...], o_gr[...]))
    put(8, tn(h2[...], gpre[...]))
    for n in range(3):
        got = tn(activ[:, n * 256 : n * 256 + 256], gout[...])
        gdown[0, n * 256 : n * 256 + 256, :] = got[:, :128]
        gdown[1, n * 256 : n * 256 + 256, :] = got[:, 128:]

    def backward(i, carry):
        _, _, r0, c0 = place(i)
        slab = slab_of(r0, c0)
        qe = expand(block_of(q, r0, c0), masks)
        ge = expand(block_of(gatt, r0, c0), masks)
        pb = probs[i]
        p = pb.astype(F32)
        gs = nt(slab[:, C:], ge)
        ds = (p * (gs - jnp.sum(p * gs, axis=0, keepdims=True))).astype(BF)
        got = pick(tn(ds, slab[:, :C]), masks) * 0.125
        dq[pl.ds(r0, 8), pl.ds(c0, 8), :] = got.reshape(8, 8, C)
        at = (pl.ds(r0, KR), pl.ds(c0, KC))
        dkv[at + (slice(0, C),)] += nn(ds, qe).reshape(KR, KC, C)
        dkv[at + (slice(C, 2 * C),)] += nn(pb, ge).reshape(KR, KC, C)
        return carry

    lax.fori_loop(0, NB, backward, 0)

    o_dq[...] = dq[...].reshape(TR * TC, C).astype(BF)
    gq = tn(h1l[...], o_dq[...])
    gkv = tn(h1e[...], dkv[...].reshape(ER * EC, 2 * C).astype(BF))
    put(0, gq)
    put(2, gkv)

    prod = gq * w_qkv[:, :C].astype(F32)
    both = gkv * w_qkv[:, C:].astype(F32)
    lanes = prod[:, :128] + prod[:, 128:]
    for n in range(4):
        lanes = lanes + both[:, n * 128 : n * 128 + 128]
    gsc1 = jnp.sum(lanes.T, axis=0, keepdims=True) / s0
    rows = [gsc1[:, :128], gsc1[:, 128:], gsc2[:, :128], gsc2[:, 128:]]

    for c in range(2):
        for j in range(2):
            for n in range(14):
                pk[c, pl.ds(j * 14 + n, 64, stride=CHUNK), :] = gmat[
                    n, pl.ds(2 * c + j, 64, stride=4), :
                ]
        for j in range(6):
            for n in range(2):
                pk[c, pl.ds(28 + j * 2 + n, 64, stride=CHUNK), :] = gdown[
                    n, pl.ds(6 * c + j, 64, stride=12), :
                ]
        for j in range(4):
            pk[c, pl.ds(40 + j, 64, stride=CHUNK), :] = jnp.broadcast_to(rows[j], (64, 128))
            pk[c, pl.ds(44 + j, 64, stride=CHUNK), :] = jnp.zeros((64, 128), F32)
    o_keep[...] = pk[core].astype(BF)
    o_send[...] = pk[1 - core].astype(BF)

    side[...] = jnp.zeros_like(side)
    for r in range(ER):
        side[0, 3 * r : 3 * r + 3, :] = dkv[r, 0:3, :]
        side[1, 3 * r : 3 * r + 3, :] = dkv[r, TC + 3 : TC + 6, :]
    o_left[...] = side[0].astype(BF)
    o_right[...] = side[1].astype(BF)
    o_top[...] = dkv[0:3, 3 : TC + 3, :].reshape(3 * TC, 2 * C).astype(BF)
    o_bottom[...] = dkv[TR + 3 :, 3 : TC + 3, :].reshape(3 * TC, 2 * C).astype(BF)
    o_core[...] = dkv[3 : TR + 3, 3 : TC + 3, :].reshape(TR * TC, 2 * C).astype(BF)


def rim_kernel(top, bottom, from_left, from_right, o_top, o_bottom, work):
    for src, dst, first in ((top, o_top, 0), (bottom, o_bottom, TR + 3)):
        work[...] = src[...].astype(F32)
        left = from_left[...].astype(F32)
        right = from_right[...].astype(F32)
        for r in range(3):
            k = 3 * (first + r)
            work[r * TC : r * TC + 3, :] += left[k : k + 3, :]
            work[r * TC + TC - 3 : r * TC + TC, :] += right[k : k + 3, :]
        dst[...] = work[...].astype(BF)


def final_kernel(
    tok,
    gr,
    dq,
    core,
    from_left,
    from_right,
    from_above,
    from_below,
    w_qkv,
    scales,
    parts,
    o_tok,
    o_qkv,
    o_out,
    o_up,
    o_down,
    o_scales,
    work,
    left,
    right,
    *,
    loss_scale,
):
    work[...] = core[...].astype(F32)
    work[0 : 3 * TC, :] += from_above[...].astype(F32)
    work[(TR - 3) * TC :, :] += from_below[...].astype(F32)
    left[...] = from_left[...].astype(F32)
    right[...] = from_right[...].astype(F32)
    for r in range(TR):
        k = 3 * (r + 3)
        work[r * TC : r * TC + 3, :] += left[k : k + 3, :]
        work[r * TC + TC - 3 : r * TC + TC, :] += right[k : k + 3, :]
    s0 = scales[0:1, :]

    def step(i, carry):
        at = pl.ds(pl.multiple_of(i * 256, 256), 256)
        gh = nt(dq[at, :], w_qkv[:, :C]) + nt(work[at, :].astype(BF), w_qkv[:, C:])
        n1, inv1 = norm(tok[at, :].astype(F32))
        gn = gh * s0
        back = inv1 * (gn - n1 * jnp.mean(gn * n1, axis=-1, keepdims=True))
        o_tok[at, :] = (gr[at, :].astype(F32) + back).astype(BF)
        return carry

    lax.fori_loop(0, 4, step, 0)

    total = parts[0].astype(F32)
    for k in range(1, 64):
        total = total + parts[k].astype(F32)
    total = total * loss_scale
    for j in range(2):
        for n in range(14):
            row = total[j * 14 + n : j * 14 + n + 1, :]
            if n < 6:
                o_qkv[j : j + 1, n * 128 : n * 128 + 128] = row
            elif n < 8:
                o_out[j : j + 1, (n - 6) * 128 : (n - 6) * 128 + 128] = row
            else:
                o_up[j : j + 1, (n - 8) * 128 : (n - 8) * 128 + 128] = row
    for j in range(6):
        for n in range(2):
            o_down[j : j + 1, n * 128 : n * 128 + 128] = total[28 + 2 * j + n : 29 + 2 * j + n, :]
    for j in range(4):
        o_scales[j // 2 : j // 2 + 1, (j % 2) * 128 : (j % 2) * 128 + 128] = total[
            40 + j : 41 + j, :
        ]


def vm(n):
    return [pl.BlockSpec(memory_space=pltpu.VMEM)] * n


def sds(shape, dtype):
    return jax.ShapeDtypeStruct(shape, dtype)


PARAMS = dict(compiler_params=pltpu.CompilerParams(vmem_limit_bytes=52 * 1024 * 1024))


def along(x, axes, by):
    size = lax.axis_size(axes)
    return lax.ppermute(x, axes, [(i, i + by) for i in range(size) if 0 <= i + by < size])


def body(tokens, grad_out, scales, w_qkv, w_out, w_up, w_down):
    rows_total = TR * lax.axis_size(ROW)
    cols_total = TC * lax.axis_size(COL)
    core_id = lax.axis_index("core")
    pos = jnp.stack([lax.axis_index(ROW) * TR, lax.axis_index(COL) * TC, core_id]).astype(jnp.int32)

    above = along(tokens[TR - 3 :], ROW, 1)
    below = along(tokens[:3], ROW, -1)
    tall = jnp.concatenate([above, tokens, below], axis=0)
    before = along(tall[:, TC - 3 :], COL, 1)
    after = along(tall[:, :3], COL, -1)
    pad = jnp.zeros((ER, EC - TC - 6, C), BF)
    tok_ext = jnp.concatenate([before, tall, after, pad], axis=1)

    flat = TR * TC
    tok = tokens.reshape(flat, C)
    gout = grad_out.reshape(flat, C)
    outs = pl.pallas_call(
        functools.partial(main_kernel, rows_total=rows_total, cols_total=cols_total),
        out_shape=[
            sds((flat, C), BF),
            sds((flat, C), BF),
            sds((flat, 2 * C), BF),
            sds((80, 2 * C), BF),
            sds((80, 2 * C), BF),
            sds((3 * TC, 2 * C), BF),
            sds((3 * TC, 2 * C), BF),
            sds((64 * CHUNK, 128), BF),
            sds((64 * CHUNK, 128), BF),
        ],
        in_specs=[pl.BlockSpec(memory_space=pltpu.SMEM)] + vm(8),
        out_specs=vm(9),
        scratch_shapes=[
            pltpu.VMEM((6, NK, 256), F32),
            pltpu.VMEM((ER, EC, 2 * C), F32),
            pltpu.VMEM((ER, EC, 2 * C), F32),
            pltpu.VMEM((TR, TC, C), F32),
            pltpu.VMEM((TR, TC, C), F32),
            pltpu.VMEM((TR, TC, C), F32),
            pltpu.VMEM((TR, TC, C), F32),
            pltpu.VMEM((NB, NK, 256), BF),
            pltpu.VMEM((ER * EC, C), BF),
            pltpu.VMEM((flat, C), BF),
            pltpu.VMEM((flat, C), BF),
            pltpu.VMEM((flat, C), BF),
            pltpu.VMEM((flat, FF), BF),
            pltpu.VMEM((flat, FF), BF),
            pltpu.VMEM((14, 256, 128), F32),
            pltpu.VMEM((2, FF, 128), F32),
            pltpu.VMEM((2, 64 * CHUNK, 128), F32),
            pltpu.VMEM((2, 80, 2 * C), F32),
            pltpu.VMEM((1, C), F32),
        ],
        name="block_backward",
        **PARAMS,
    )(pos, tok_ext, tok, gout, scales, w_qkv, w_out, w_up, w_down)
    gr, dq, core, left, right, top, bottom, keep, send = outs

    from_right = along(left, COL, -1)
    from_left = along(right, COL, 1)
    got = lax.ppermute(send, "core", [(0, 1), (1, 0)])
    top, bottom = pl.pallas_call(
        rim_kernel,
        out_shape=[sds((3 * TC, 2 * C), BF)] * 2,
        in_specs=vm(4),
        out_specs=vm(2),
        scratch_shapes=[pltpu.VMEM((3 * TC, 2 * C), F32)],
        name="rims",
        **PARAMS,
    )(top, bottom, from_left, from_right)
    from_below = along(top, ROW, -1)
    from_above = along(bottom, ROW, 1)
    mine = (keep + got).reshape(64, CHUNK, 128)
    parts = lax.all_to_all(mine, CHIPS, 0, 0, tiled=True)

    outs = pl.pallas_call(
        functools.partial(final_kernel, loss_scale=1.0 / math.sqrt(rows_total * cols_total)),
        out_shape=[
            sds((flat, C), BF),
            sds((2, 3 * C), F32),
            sds((2, C), F32),
            sds((2, FF), F32),
            sds((6, C), F32),
            sds((2, C), F32),
        ],
        in_specs=vm(11),
        out_specs=vm(6),
        scratch_shapes=[
            pltpu.VMEM((flat, 2 * C), F32),
            pltpu.VMEM((80, 2 * C), F32),
            pltpu.VMEM((80, 2 * C), F32),
        ],
        name="grad_tokens",
        **PARAMS,
    )(tok, gr, dq, core, from_left, from_right, from_above, from_below, w_qkv, scales, parts)
    return (outs[0].reshape(TR, TC, C),) + tuple(outs[1:])


def solution(mesh):
    fine = Mesh(mesh.devices.reshape(4, 2, 4, 2, 2), ("x", "zh", "y", "zl", "core"))
    tile = P(ROW, COL, None)
    share = P(ROW + COL, None)
    return jax.shard_map(
        body,
        mesh=fine,
        in_specs=(tile, tile, P(), P(), P(), P(), P()),
        out_specs=(tile, share, share, share, share, P()),
        check_vma=False,
    )
```

```python
import functools
import math

import jax
import jax.numpy as jnp
from jax import lax
from jax.experimental import pallas as pl
from jax.experimental.pallas import tpu as pltpu
from jax.sharding import Mesh, PartitionSpec as P

HEADS = 4
C = 256
FF = 768
TR, TC = 16, 64
ER, EC = 22, 72
KR, KC = 14, 16
NK = KR * KC
NB = 16
CHUNK = 48
EPS = 1e-6
NEG = -1e30
BF = jnp.bfloat16
F32 = jnp.float32
GA = math.sqrt(2.0 / math.pi)
GB = GA * 0.044715

ROW = ("x", "zh")
COL = ("y", "zl", "core")
CHIPS = ("x", "zh", "y", "zl")


def nt(a, b):
    return lax.dot_general(a, b, (((1,), (1,)), ((), ())), preferred_element_type=F32)


def tn(a, b):
    return lax.dot_general(a, b, (((0,), (0,)), ((), ())), preferred_element_type=F32)


def nn(a, b):
    return jnp.dot(a, b, preferred_element_type=F32)


def norm(x):
    inverse = lax.rsqrt(jnp.mean(x * x, axis=-1, keepdims=True) + EPS)
    return x * inverse, inverse


def head_masks():
    lane = lax.broadcasted_iota(jnp.int32, (1, C), 1)
    return [(jnp.right_shift(lane, 6) == h).astype(F32) for h in range(HEADS)]


def expand(x, masks):
    return jnp.concatenate([x * m for m in masks], axis=0).astype(BF)


def pick(x, masks):
    out = x[0:64] * masks[0]
    for h in range(1, HEADS):
        out = out + x[64 * h : 64 * h + 64] * masks[h]
    return out


def main_kernel(
    pos,
    tok,
    gout,
    intra,
    inter,
    first,
    second,
    scales,
    w_qkv,
    w_out,
    w_up,
    w_down,
    o_gr,
    o_gh,
    o_intra,
    o_inter,
    o_top,
    o_bottom,
    o_keep,
    o_send,
    bias,
    kv,
    dkv,
    q,
    att,
    gatt,
    dq,
    probs,
    h1l,
    attb,
    h2,
    activ,
    gpre,
    gmat,
    gdown,
    pk,
    side_in,
    side,
    *,
    rows_total,
    cols_total,
):
    base_r, base_c, core, half_row = pos[0], pos[1], pos[2], pos[3]
    even = core == 0
    masks = head_masks()

    key = lax.broadcasted_iota(jnp.int32, (NK, 1), 0)
    lane = jnp.bitwise_and(lax.broadcasted_iota(jnp.int32, (1, 256), 1), 63)
    for rb in range(2):
        k_row = base_r + rb * 8 - 3 + jnp.right_shift(key, 4)
        q_row = base_r + rb * 8 + jnp.right_shift(lane, 3)
        s_row = jnp.clip(q_row - 3, 0, rows_total - 7)
        row_ok = (k_row >= s_row) & (k_row <= s_row + 6)
        for kind, c0 in enumerate((0, 8, 56)):
            k_col = base_c + c0 - 3 + jnp.bitwise_and(key, 15)
            q_col = base_c + c0 + jnp.bitwise_and(lane, 7)
            s_col = jnp.clip(q_col - 3, 0, cols_total - 7)
            ok = row_ok & (k_col >= s_col) & (k_col <= s_col + 6)
            bias[rb * 3 + kind] = jnp.where(ok, 0.0, NEG)

    s0 = scales[0:1, :]
    s1 = scales[1:2, :]

    def hidden(x):
        return (norm(x.astype(F32))[0] * s0).astype(BF)

    kv[:, TC:, :] = jnp.zeros((ER, EC - TC, 2 * C), F32)
    for i in range(4):
        at = slice(256 * i, 256 * i + 256)
        h = hidden(tok[at, :])
        h1l[at, :] = h
        got = nn(h, w_qkv[:, :C]).astype(BF).astype(F32) * 0.125
        q[4 * i : 4 * i + 4] = got.reshape(4, TC, C)
        got = nn(h, w_qkv[:, C:])
        kv[3 + 4 * i : 7 + 4 * i, 3 : TC + 3, :] = got.reshape(4, TC, 2 * C)

    side_in[...] = jnp.zeros_like(side_in)
    upper = half_row == 0
    one = first[...].astype(F32)
    two = second[...].astype(F32)
    h_rows = []
    for at, x in ((0, jnp.where(upper, two, one)), (TR + 3, jnp.where(upper, one, two))):
        h = hidden(x[0 : 3 * TC])
        h_rows.append(h)
        kv[at : at + 3, 3 : TC + 3, :] = nn(h, w_qkv[:, C:]).reshape(3, TC, 2 * C)
        for k in range(2):
            lo = 3 * TC + 16 * k
            side_in[k, 3 * at : 3 * at + 9, :] = x[lo : lo + 9]
    h_above, h_below = h_rows
    for r in range(TR):
        near = intra[r].astype(F32)
        far = inter[r].astype(F32)
        side_in[0, 3 * r + 9 : 3 * r + 12, :] = jnp.where(even, far, near)
        side_in[1, 3 * r + 9 : 3 * r + 12, :] = jnp.where(even, near, far)
    h_side = [hidden(side_in[k]) for k in range(2)]
    for k in range(2):
        got = nn(h_side[k], w_qkv[:, C:])
        lo = k * (TC + 3)
        for r in range(ER):
            kv[r, lo : lo + 3, :] = got[3 * r : 3 * r + 3, :]
    dkv[...] = jnp.zeros_like(dkv)

    blocks = [(rb, cb) for cb in range(8) for rb in range(2)]

    def block_of(ref, r0, c0):
        return ref[r0 : r0 + 8, c0 : c0 + 8, :].reshape(64, C)

    def slab_of(r0, c0):
        return kv[r0 : r0 + KR, c0 : c0 + KC, :].astype(BF).reshape(NK, 2 * C)

    for i, (rb, cb) in enumerate(blocks):
        r0, c0 = 8 * rb, 8 * cb
        slab = slab_of(r0, c0)
        qe = expand(block_of(q, r0, c0), masks)
        kind = 0 if cb == 0 else 2 if cb == 7 else 1
        s = nt(slab[:, :C], qe) + bias[rb * 3 + kind]
        e = jnp.exp(s - jnp.max(s, axis=0, keepdims=True))
        p = (e * (1.0 / jnp.sum(e, axis=0, keepdims=True))).astype(BF)
        probs[i] = p
        out = pick(tn(p, slab[:, C:]), masks)
        att[r0 : r0 + 8, c0 : c0 + 8, :] = out.reshape(8, 8, C)

    gsc2 = jnp.zeros((1, C), F32)
    for i in range(4):
        at = slice(256 * i, 256 * i + 256)
        a = att[4 * i : 4 * i + 4].reshape(256, C).astype(BF)
        attb[at, :] = a
        resid = (tok[at, :].astype(F32) + nn(a, w_out[...])).astype(BF).astype(F32)
        n2, inv2 = norm(resid)
        h = (n2 * s1).astype(BF)
        h2[at, :] = h
        x = nn(h, w_up[...])
        g = gout[at, :]
        ga = nt(g, w_down[...])
        xx = x * x
        t = jnp.tanh(x * (GA + GB * xx))
        half = 0.5 + 0.5 * t
        act = x * half
        activ[at, :] = act.astype(BF)
        gp = (ga * (half + act * (1.0 - t) * (GA + (3.0 * GB) * xx))).astype(BF)
        gpre[at, :] = gp
        gh = nt(gp, w_up[...])
        gn = gh * s1
        back = inv2 * (gn - n2 * jnp.mean(gn * n2, axis=-1, keepdims=True))
        gsc2 = gsc2 + jnp.sum(gh * n2, axis=0, keepdims=True)
        gr = (g.astype(F32) + back).astype(BF)
        o_gr[at, :] = gr
        gatt[4 * i : 4 * i + 4] = nt(gr, w_out[...]).astype(BF).astype(F32).reshape(4, TC, C)

    def put(first, value):
        for n in range(value.shape[1] // 128):
            gmat[first + n] = value[:, n * 128 : n * 128 + 128]

    put(6, tn(attb[...], o_gr[...]))
    put(8, tn(h2[...], gpre[...]))
    for n in range(3):
        got = tn(activ[:, n * 256 : n * 256 + 256], gout[...])
        gdown[0, n * 256 : n * 256 + 256, :] = got[:, :128]
        gdown[1, n * 256 : n * 256 + 256, :] = got[:, 128:]

    for i, (rb, cb) in enumerate(blocks):
        r0, c0 = 8 * rb, 8 * cb
        slab = slab_of(r0, c0)
        qe = expand(block_of(q, r0, c0), masks)
        ge = expand(block_of(gatt, r0, c0), masks)
        pb = probs[i]
        p = pb.astype(F32)
        gs = nt(slab[:, C:], ge)
        ds = (p * (gs - jnp.sum(p * gs, axis=0, keepdims=True))).astype(BF)
        got = pick(tn(ds, slab[:, :C]), masks) * 0.125
        dq[r0 : r0 + 8, c0 : c0 + 8, :] = got.reshape(8, 8, C)
        dkv[r0 : r0 + KR, c0 : c0 + KC, :C] += nn(ds, qe).reshape(KR, KC, C)
        dkv[r0 : r0 + KR, c0 : c0 + KC, C:] += nn(pb, ge).reshape(KR, KC, C)

    side[...] = jnp.zeros_like(side)
    for r in range(ER):
        side[0, 3 * r : 3 * r + 3, :] = dkv[r, 0:3, :]
        side[1, 3 * r : 3 * r + 3, :] = dkv[r, TC + 3 : TC + 6, :]
    top = dkv[0:3, 3 : TC + 3, :].reshape(3 * TC, 2 * C).astype(BF)
    bottom = dkv[TR + 3 :, 3 : TC + 3, :].reshape(3 * TC, 2 * C).astype(BF)
    left = side[0].astype(BF)
    right = side[1].astype(BF)
    g_left = nt(left, w_qkv[:, C:])
    g_right = nt(right, w_qkv[:, C:])
    o_intra[...] = jnp.where(even, g_right, g_left).astype(BF)
    o_inter[...] = jnp.where(even, g_left, g_right).astype(BF)
    o_top[...] = nt(top, w_qkv[:, C:])
    o_bottom[...] = nt(bottom, w_qkv[:, C:])

    gq = jnp.zeros((C, C), F32)
    gkv = tn(h_above, top) + tn(h_below, bottom) + tn(h_side[0], left) + tn(h_side[1], right)
    for i in range(4):
        at = slice(256 * i, 256 * i + 256)
        d_q = dq[4 * i : 4 * i + 4].reshape(256, C).astype(BF)
        d_kv = dkv[3 + 4 * i : 7 + 4 * i, 3 : TC + 3, :].reshape(256, 2 * C).astype(BF)
        o_gh[at, :] = nt(d_q, w_qkv[:, :C]) + nt(d_kv, w_qkv[:, C:])
        h = h1l[at, :]
        gq = gq + tn(h, d_q)
        gkv = gkv + tn(h, d_kv)
    put(0, gq)
    put(2, gkv)

    prod = gq * w_qkv[:, :C].astype(F32)
    both = gkv * w_qkv[:, C:].astype(F32)
    lanes = prod[:, :128] + prod[:, 128:]
    for n in range(4):
        lanes = lanes + both[:, n * 128 : n * 128 + 128]
    gsc1 = jnp.sum(lanes.T, axis=0, keepdims=True) / s0
    rows = [gsc1[:, :128], gsc1[:, 128:], gsc2[:, :128], gsc2[:, 128:]]

    for c in range(2):
        for j in range(2):
            for n in range(14):
                pk[c, pl.ds(j * 14 + n, 64, stride=CHUNK), :] = gmat[
                    n, pl.ds(2 * c + j, 64, stride=4), :
                ]
        for j in range(6):
            for n in range(2):
                pk[c, pl.ds(28 + j * 2 + n, 64, stride=CHUNK), :] = gdown[
                    n, pl.ds(6 * c + j, 64, stride=12), :
                ]
        for j in range(4):
            pk[c, pl.ds(40 + j, 64, stride=CHUNK), :] = jnp.broadcast_to(rows[j], (64, 128))
            pk[c, pl.ds(44 + j, 64, stride=CHUNK), :] = jnp.zeros((64, 128), F32)
    o_keep[...] = pk[core].astype(BF)
    o_send[...] = pk[1 - core].astype(BF)


def rim_kernel(
    pos, top, bottom, intra, inter, keep, got, o_first, o_second, o_mine, work
):
    even = pos[2] == 0
    upper = pos[3] == 0
    near = intra[...].astype(F32)
    far = inter[...].astype(F32)
    left = jnp.where(even, far, near)
    right = jnp.where(even, near, far)
    for n, (src, at) in enumerate(((top, 0), (bottom, TR + 3))):
        work[n] = src[...]
        for r in range(3):
            k = 3 * (at + r)
            work[n, r * TC : r * TC + 3, :] += left[k : k + 3, :]
            work[n, r * TC + TC - 3 : r * TC + TC, :] += right[k : k + 3, :]
    o_first[...] = jnp.where(upper, work[1], work[0]).astype(BF)
    o_second[...] = jnp.where(upper, work[0], work[1]).astype(BF)
    o_mine[...] = (keep[...].astype(F32) + got[...].astype(F32)).astype(BF)


def token_kernel(pos, tok, gr, gh, intra, inter, first, second, scales, o_tok, work):
    even = pos[2] == 0
    upper = pos[3] == 0
    near = intra[...].astype(F32)
    far = inter[...].astype(F32)
    left = jnp.where(even, far, near)
    right = jnp.where(even, near, far)
    work[...] = gh[...]
    one = first[...].astype(F32)
    two = second[...].astype(F32)
    work[0 : 3 * TC, :] += jnp.where(upper, two, one)
    work[(TR - 3) * TC :, :] += jnp.where(upper, one, two)
    for r in range(TR):
        k = 3 * (r + 3)
        work[r * TC : r * TC + 3, :] += left[k : k + 3, :]
        work[r * TC + TC - 3 : r * TC + TC, :] += right[k : k + 3, :]
    s0 = scales[0:1, :]
    for i in range(4):
        at = slice(256 * i, 256 * i + 256)
        n1, inv1 = norm(tok[at, :].astype(F32))
        gn = work[at, :] * s0
        back = inv1 * (gn - n1 * jnp.mean(gn * n1, axis=-1, keepdims=True))
        o_tok[at, :] = (gr[at, :].astype(F32) + back).astype(BF)


def sum_kernel(parts, o_qkv, o_out, o_up, o_down, o_scales, *, loss_scale):
    total = parts[0].astype(F32)
    for k in range(1, 64):
        total = total + parts[k].astype(F32)
    total = total * loss_scale
    for j in range(2):
        for n in range(14):
            row = total[j * 14 + n : j * 14 + n + 1, :]
            if n < 6:
                o_qkv[j : j + 1, n * 128 : n * 128 + 128] = row
            elif n < 8:
                o_out[j : j + 1, (n - 6) * 128 : (n - 6) * 128 + 128] = row
            else:
                o_up[j : j + 1, (n - 8) * 128 : (n - 8) * 128 + 128] = row
    for j in range(6):
        for n in range(2):
            o_down[j : j + 1, n * 128 : n * 128 + 128] = total[28 + 2 * j + n : 29 + 2 * j + n, :]
    for j in range(4):
        o_scales[j // 2 : j // 2 + 1, (j % 2) * 128 : (j % 2) * 128 + 128] = total[
            40 + j : 41 + j, :
        ]


def vm(n):
    return [pl.BlockSpec(memory_space=pltpu.VMEM)] * n


def sds(shape, dtype):
    return jax.ShapeDtypeStruct(shape, dtype)


def params(mib):
    return dict(compiler_params=pltpu.CompilerParams(vmem_limit_bytes=mib * 1024 * 1024))


def swap(x, axes, odd):
    size = lax.axis_size(axes)
    pairs = [(i, i + 1) for i in range(odd, size - 1, 2)]
    return lax.ppermute(x, axes, pairs + [(b, a) for a, b in pairs])


def body(tokens, grad_out, scales, w_qkv, w_out, w_up, w_down):
    rows_total = TR * lax.axis_size(ROW)
    cols_total = TC * lax.axis_size(COL)
    core_id = lax.axis_index("core")
    half_row = lax.axis_index("zh")
    pos = jnp.stack(
        [lax.axis_index(ROW) * TR, lax.axis_index(COL) * TC, core_id, half_row]
    ).astype(jnp.int32)
    flat = TR * TC
    tok = tokens.reshape(flat, C)
    gout = grad_out.reshape(flat, C)
    smem = [pl.BlockSpec(memory_space=pltpu.SMEM)]

    even, upper = core_id == 0, half_row == 0
    head, tail = tokens[:, :3], tokens[:, TC - 3 :]
    inter = swap(jnp.where(even, head, tail), COL, 1)
    intra = swap(jnp.where(even, tail, head), COL, 0)
    before = jnp.where(even, inter, intra)
    after = jnp.where(even, intra, inter)

    def rim(lo):
        gap = jnp.zeros((7, C), BF)
        return jnp.concatenate(
            [
                tok[lo * TC : (lo + 3) * TC],
                before[lo : lo + 3].reshape(9, C),
                gap,
                after[lo : lo + 3].reshape(9, C),
                gap,
            ],
            axis=0,
        )

    top, bottom = rim(0), rim(TR - 3)
    first = swap(jnp.where(upper, bottom, top), ROW, 0)
    second = swap(jnp.where(upper, top, bottom), ROW, 1)

    outs = pl.pallas_call(
        functools.partial(main_kernel, rows_total=rows_total, cols_total=cols_total),
        out_shape=[
            sds((flat, C), BF),
            sds((flat, C), F32),
            sds((80, C), BF),
            sds((80, C), BF),
            sds((3 * TC, C), F32),
            sds((3 * TC, C), F32),
            sds((64 * CHUNK, 128), BF),
            sds((64 * CHUNK, 128), BF),
        ],
        in_specs=smem + vm(11),
        out_specs=vm(8),
        scratch_shapes=[
            pltpu.VMEM((6, NK, 256), F32),
            pltpu.VMEM((ER, EC, 2 * C), F32),
            pltpu.VMEM((ER, EC, 2 * C), F32),
            pltpu.VMEM((TR, TC, C), F32),
            pltpu.VMEM((TR, TC, C), F32),
            pltpu.VMEM((TR, TC, C), F32),
            pltpu.VMEM((TR, TC, C), F32),
            pltpu.VMEM((NB, NK, 256), BF),
            pltpu.VMEM((flat, C), BF),
            pltpu.VMEM((flat, C), BF),
            pltpu.VMEM((flat, C), BF),
            pltpu.VMEM((flat, FF), BF),
            pltpu.VMEM((flat, FF), BF),
            pltpu.VMEM((14, 256, 128), F32),
            pltpu.VMEM((2, FF, 128), F32),
            pltpu.VMEM((2, 64 * CHUNK, 128), F32),
            pltpu.VMEM((2, 80, C), F32),
            pltpu.VMEM((2, 80, 2 * C), F32),
        ],
        name="block_backward",
        **params(44),
    )(pos, tok, gout, intra, inter, first, second, scales, w_qkv, w_out, w_up, w_down)
    gr, gh, g_intra, g_inter, top, bottom, keep, send = outs

    inter = swap(g_inter, COL, 1)
    intra = swap(g_intra, COL, 0)
    got = lax.ppermute(send, "core", [(0, 1), (1, 0)])
    first, second, mine = pl.pallas_call(
        rim_kernel,
        out_shape=[sds((3 * TC, C), BF)] * 2 + [sds((64 * CHUNK, 128), BF)],
        in_specs=smem + vm(6),
        out_specs=vm(3),
        scratch_shapes=[pltpu.VMEM((2, 3 * TC, C), F32)],
        name="rims",
        **params(16),
    )(pos, top, bottom, intra, inter, keep, got)
    first = swap(first, ROW, 0)
    second = swap(second, ROW, 1)
    parts = lax.all_to_all(mine.reshape(64, CHUNK, 128), CHIPS, 0, 0, tiled=True)
    grad_tokens = pl.pallas_call(
        token_kernel,
        out_shape=sds((flat, C), BF),
        in_specs=smem + vm(8),
        out_specs=vm(1)[0],
        scratch_shapes=[pltpu.VMEM((flat, C), F32)],
        cost_estimate=pl.CostEstimate(
            flops=30 * flat * C, bytes_accessed=10 * flat * C, transcendentals=0
        ),
        name="grad_tokens",
        **params(16),
    )(pos, tok, gr, gh, intra, inter, first, second, scales)
    outs = pl.pallas_call(
        functools.partial(sum_kernel, loss_scale=1.0 / math.sqrt(rows_total * cols_total)),
        out_shape=[
            sds((2, 3 * C), F32),
            sds((2, C), F32),
            sds((2, FF), F32),
            sds((6, C), F32),
            sds((2, C), F32),
        ],
        in_specs=vm(1),
        out_specs=vm(5),
        name="weight_sums",
        **params(16),
    )(parts)
    return (grad_tokens.reshape(TR, TC, C),) + tuple(outs)


def solution(mesh):
    fine = Mesh(mesh.devices.reshape(4, 2, 4, 2, 2), ("x", "zh", "y", "zl", "core"))
    tile = P(ROW, COL, None)
    share = P(ROW + COL, None)
    return jax.shard_map(
        body,
        mesh=fine,
        in_specs=(tile, tile, P(), P(), P(), P(), P()),
        out_specs=(tile, share, share, share, share, P()),
        check_vma=False,
    )
```

```python
import functools
import math

import jax
import jax.numpy as jnp
from jax import lax
from jax.experimental import pallas as pl
from jax.experimental.pallas import tpu as pltpu
from jax.sharding import Mesh, PartitionSpec as P

HEADS = 4
C = 256
FF = 768
TR, TC = 16, 64
ER, EC = 22, 72
KR, KC = 14, 16
NK = KR * KC
NB = 16
CHUNK = 48
EPS = 1e-6
NEG = -1e30
BF = jnp.bfloat16
F32 = jnp.float32
GA = math.sqrt(2.0 / math.pi)
GB = GA * 0.044715

ROW = ("x", "zh")
COL = ("y", "zl", "core")
CHIPS = ("x", "zh", "y", "zl")


def nt(a, b):
    return lax.dot_general(a, b, (((1,), (1,)), ((), ())), preferred_element_type=F32)


def tn(a, b):
    return lax.dot_general(a, b, (((0,), (0,)), ((), ())), preferred_element_type=F32)


def nn(a, b):
    return jnp.dot(a, b, preferred_element_type=F32)


def norm(x):
    inverse = lax.rsqrt(jnp.mean(x * x, axis=-1, keepdims=True) + EPS)
    return x * inverse, inverse


def head_masks():
    lane = lax.broadcasted_iota(jnp.int32, (1, C), 1)
    return [(jnp.right_shift(lane, 6) == h).astype(F32) for h in range(HEADS)]


def expand(x, masks):
    return jnp.concatenate([x * m for m in masks], axis=0).astype(BF)


def pick(x, masks):
    out = x[0:64] * masks[0]
    for h in range(1, HEADS):
        out = out + x[64 * h : 64 * h + 64] * masks[h]
    return out


def main_kernel(
    pos,
    tok,
    gout,
    intra,
    inter,
    first,
    second,
    scales,
    w_wide,
    w_tall,
    o_gr,
    o_gh,
    o_intra,
    o_inter,
    o_first,
    o_second,
    o_keep,
    o_send,
    bias,
    kv,
    dkv,
    q,
    att,
    gatt,
    dq,
    probs,
    h1l,
    attb,
    h2,
    activ,
    gpre,
    gmat,
    gdown,
    pk,
    side_in,
    side,
    *,
    rows_total,
    cols_total,
):
    base_r, base_c, core, half_row = pos[0], pos[1], pos[2], pos[3]
    even = core == 0
    masks = head_masks()
    w_qkv, w_up = w_wide.at[0:C], w_wide.at[C : 2 * C]
    w_out, w_down = w_tall.at[0:C], w_tall.at[C : C + FF]

    key = lax.broadcasted_iota(jnp.int32, (NK, 1), 0)
    lane = jnp.bitwise_and(lax.broadcasted_iota(jnp.int32, (1, 256), 1), 63)
    for rb in range(2):
        k_row = base_r + rb * 8 - 3 + jnp.right_shift(key, 4)
        q_row = base_r + rb * 8 + jnp.right_shift(lane, 3)
        s_row = jnp.clip(q_row - 3, 0, rows_total - 7)
        row_ok = (k_row >= s_row) & (k_row <= s_row + 6)
        for kind, c0 in enumerate((0, 8, 56)):
            k_col = base_c + c0 - 3 + jnp.bitwise_and(key, 15)
            q_col = base_c + c0 + jnp.bitwise_and(lane, 7)
            s_col = jnp.clip(q_col - 3, 0, cols_total - 7)
            ok = row_ok & (k_col >= s_col) & (k_col <= s_col + 6)
            bias[rb * 3 + kind] = jnp.where(ok, 0.0, NEG)

    s0 = scales[0:1, :]
    s1 = scales[1:2, :]

    def hidden(x):
        return (norm(x.astype(F32))[0] * s0).astype(BF)

    kv[:, TC:, :] = jnp.zeros((ER, EC - TC, 2 * C), F32)
    for i in range(4):
        at = slice(256 * i, 256 * i + 256)
        h = hidden(tok[at, :])
        h1l[at, :] = h
        got = nn(h, w_qkv[:, :C]).astype(BF).astype(F32) * 0.125
        q[4 * i : 4 * i + 4] = got.reshape(4, TC, C)
        got = nn(h, w_qkv[:, C:])
        kv[3 + 4 * i : 7 + 4 * i, 3 : TC + 3, :] = got.reshape(4, TC, 2 * C)

    side_in[...] = jnp.zeros_like(side_in)
    upper = half_row == 0
    one = first[...].astype(F32)
    two = second[...].astype(F32)
    h_rows = []
    for at, x in ((0, jnp.where(upper, two, one)), (TR + 3, jnp.where(upper, one, two))):
        h = hidden(x[0 : 3 * TC])
        h_rows.append(h)
        kv[at : at + 3, 3 : TC + 3, :] = nn(h, w_qkv[:, C:]).reshape(3, TC, 2 * C)
        for k in range(2):
            lo = 3 * TC + 16 * k
            side_in[k, 3 * at : 3 * at + 9, :] = x[lo : lo + 9]
    h_above, h_below = h_rows
    for r in range(TR):
        near = intra[r].astype(F32)
        far = inter[r].astype(F32)
        side_in[0, 3 * r + 9 : 3 * r + 12, :] = jnp.where(even, far, near)
        side_in[1, 3 * r + 9 : 3 * r + 12, :] = jnp.where(even, near, far)
    h_side = [hidden(side_in[k]) for k in range(2)]
    for k in range(2):
        got = nn(h_side[k], w_qkv[:, C:])
        lo = k * (TC + 3)
        for r in range(ER):
            kv[r, lo : lo + 3, :] = got[3 * r : 3 * r + 3, :]
    dkv[...] = jnp.zeros_like(dkv)

    blocks = [(rb, cb) for cb in range(8) for rb in range(2)]

    def block_of(ref, r0, c0):
        return ref[r0 : r0 + 8, c0 : c0 + 8, :].reshape(64, C)

    def slab_of(r0, c0):
        return kv[r0 : r0 + KR, c0 : c0 + KC, :].astype(BF).reshape(NK, 2 * C)

    for i, (rb, cb) in enumerate(blocks):
        r0, c0 = 8 * rb, 8 * cb
        slab = slab_of(r0, c0)
        qe = expand(block_of(q, r0, c0), masks)
        kind = 0 if cb == 0 else 2 if cb == 7 else 1
        s = nt(slab[:, :C], qe) + bias[rb * 3 + kind]
        e = jnp.exp(s - jnp.max(s, axis=0, keepdims=True))
        p = (e * (1.0 / jnp.sum(e, axis=0, keepdims=True))).astype(BF)
        probs[i] = p
        out = pick(tn(p, slab[:, C:]), masks)
        att[r0 : r0 + 8, c0 : c0 + 8, :] = out.reshape(8, 8, C)

    gsc2 = jnp.zeros((1, C), F32)
    for i in range(4):
        at = slice(256 * i, 256 * i + 256)
        a = att[4 * i : 4 * i + 4].reshape(256, C).astype(BF)
        attb[at, :] = a
        resid = (tok[at, :].astype(F32) + nn(a, w_out[...])).astype(BF).astype(F32)
        n2, inv2 = norm(resid)
        h = (n2 * s1).astype(BF)
        h2[at, :] = h
        x = nn(h, w_up[...])
        g = gout[at, :]
        ga = nt(g, w_down[...])
        xx = x * x
        t = jnp.tanh(x * (GA + GB * xx))
        half = 0.5 + 0.5 * t
        act = x * half
        activ[at, :] = act.astype(BF)
        gp = (ga * (half + act * (1.0 - t) * (GA + (3.0 * GB) * xx))).astype(BF)
        gpre[at, :] = gp
        gh = nt(gp, w_up[...])
        gn = gh * s1
        back = inv2 * (gn - n2 * jnp.mean(gn * n2, axis=-1, keepdims=True))
        gsc2 = gsc2 + jnp.sum(gh * n2, axis=0, keepdims=True)
        gr = (g.astype(F32) + back).astype(BF)
        o_gr[at, :] = gr
        gatt[4 * i : 4 * i + 4] = nt(gr, w_out[...]).astype(BF).astype(F32).reshape(4, TC, C)

    def put(first, value):
        for n in range(value.shape[1] // 128):
            gmat[first + n] = value[:, n * 128 : n * 128 + 128]

    put(6, tn(attb[...], o_gr[...]))
    put(8, tn(h2[...], gpre[...]))
    for n in range(3):
        got = tn(activ[:, n * 256 : n * 256 + 256], gout[...])
        gdown[0, n * 256 : n * 256 + 256, :] = got[:, :128]
        gdown[1, n * 256 : n * 256 + 256, :] = got[:, 128:]

    for i, (rb, cb) in enumerate(blocks):
        r0, c0 = 8 * rb, 8 * cb
        slab = slab_of(r0, c0)
        qe = expand(block_of(q, r0, c0), masks)
        ge = expand(block_of(gatt, r0, c0), masks)
        pb = probs[i]
        p = pb.astype(F32)
        gs = nt(slab[:, C:], ge)
        ds = (p * (gs - jnp.sum(p * gs, axis=0, keepdims=True))).astype(BF)
        got = pick(tn(ds, slab[:, :C]), masks) * 0.125
        dq[r0 : r0 + 8, c0 : c0 + 8, :] = got.reshape(8, 8, C)
        dkv[r0 : r0 + KR, c0 : c0 + KC, :C] += nn(ds, qe).reshape(KR, KC, C)
        dkv[r0 : r0 + KR, c0 : c0 + KC, C:] += nn(pb, ge).reshape(KR, KC, C)

    side[...] = jnp.zeros_like(side)
    for r in range(ER):
        side[0, 3 * r : 3 * r + 3, :] = dkv[r, 0:3, :]
        side[1, 3 * r : 3 * r + 3, :] = dkv[r, TC + 3 : TC + 6, :]
    top = dkv[0:3, 3 : TC + 3, :].reshape(3 * TC, 2 * C).astype(BF)
    bottom = dkv[TR + 3 :, 3 : TC + 3, :].reshape(3 * TC, 2 * C).astype(BF)
    left = side[0].astype(BF)
    right = side[1].astype(BF)
    g_left = nt(left, w_qkv[:, C:])
    g_right = nt(right, w_qkv[:, C:])
    o_intra[...] = jnp.where(even, g_right, g_left).astype(BF)
    o_inter[...] = jnp.where(even, g_left, g_right).astype(BF)
    g_top = nt(top, w_qkv[:, C:])
    g_bottom = nt(bottom, w_qkv[:, C:])
    o_first[...] = jnp.where(upper, g_bottom, g_top).astype(BF)
    o_second[...] = jnp.where(upper, g_top, g_bottom).astype(BF)

    gq = jnp.zeros((C, C), F32)
    gkv = tn(h_above, top) + tn(h_below, bottom) + tn(h_side[0], left) + tn(h_side[1], right)
    for i in range(4):
        at = slice(256 * i, 256 * i + 256)
        d_q = dq[4 * i : 4 * i + 4].reshape(256, C).astype(BF)
        d_kv = dkv[3 + 4 * i : 7 + 4 * i, 3 : TC + 3, :].reshape(256, 2 * C).astype(BF)
        o_gh[at, :] = nt(d_q, w_qkv[:, :C]) + nt(d_kv, w_qkv[:, C:])
        h = h1l[at, :]
        gq = gq + tn(h, d_q)
        gkv = gkv + tn(h, d_kv)
    put(0, gq)
    put(2, gkv)

    prod = gq * w_qkv[:, :C].astype(F32)
    both = gkv * w_qkv[:, C:].astype(F32)
    lanes = prod[:, :128] + prod[:, 128:]
    for n in range(4):
        lanes = lanes + both[:, n * 128 : n * 128 + 128]
    gsc1 = jnp.sum(lanes.T, axis=0, keepdims=True) / s0
    rows = [gsc1[:, :128], gsc1[:, 128:], gsc2[:, :128], gsc2[:, 128:]]

    for c in range(2):
        for j in range(2):
            for n in range(14):
                pk[c, pl.ds(j * 14 + n, 64, stride=CHUNK), :] = gmat[
                    n, pl.ds(2 * c + j, 64, stride=4), :
                ]
        for j in range(6):
            for n in range(2):
                pk[c, pl.ds(28 + j * 2 + n, 64, stride=CHUNK), :] = gdown[
                    n, pl.ds(6 * c + j, 64, stride=12), :
                ]
        for j in range(4):
            pk[c, pl.ds(40 + j, 64, stride=CHUNK), :] = jnp.broadcast_to(rows[j], (64, 128))
            pk[c, pl.ds(44 + j, 64, stride=CHUNK), :] = jnp.zeros((64, 128), F32)
    o_keep[...] = pk[core].astype(BF)
    o_send[...] = pk[1 - core].astype(BF)


def add_kernel(keep, got, o_mine):
    o_mine[...] = (keep[...].astype(F32) + got[...].astype(F32)).astype(BF)


def sides_of(pos, intra, inter):
    even = pos[2] == 0
    near = intra[...].astype(F32)
    far = inter[...].astype(F32)
    return jnp.where(even, far, near), jnp.where(even, near, far)


def corner_kernel(pos, intra, inter, _first, _second, o_first, o_second, work):
    upper = pos[3] == 0
    work[...] = jnp.zeros_like(work)
    for k, x in enumerate(sides_of(pos, intra, inter)):
        work[0, 16 * k : 16 * k + 9, :] = x[0:9]
        work[1, 16 * k : 16 * k + 9, :] = x[3 * (TR + 3) : 3 * ER]
    o_first[...] = jnp.where(upper, work[1], work[0]).astype(BF)
    o_second[...] = jnp.where(upper, work[0], work[1]).astype(BF)


def token_kernel(
    pos, tok, gr, gh, intra, inter, first, second, c_first, c_second, scales, o_tok, work
):
    upper = pos[3] == 0
    left, right = sides_of(pos, intra, inter)
    work[...] = gh[...]
    one = first[...].astype(F32)
    two = second[...].astype(F32)
    work[0 : 3 * TC, :] += jnp.where(upper, two, one)
    work[(TR - 3) * TC :, :] += jnp.where(upper, one, two)
    one = c_first[...].astype(F32)
    two = c_second[...].astype(F32)
    corners = jnp.where(upper, two, one), jnp.where(upper, one, two)
    for r in range(TR):
        k = 3 * (r + 3)
        add_left, add_right = left[k : k + 3, :], right[k : k + 3, :]
        if r < 3 or r >= TR - 3:
            n, j = (0, 3 * r) if r < 3 else (1, 3 * (r - TR + 3))
            add_left = add_left + corners[n][j : j + 3, :]
            add_right = add_right + corners[n][16 + j : 19 + j, :]
        work[r * TC : r * TC + 3, :] += add_left
        work[r * TC + TC - 3 : r * TC + TC, :] += add_right
    s0 = scales[0:1, :]
    for i in range(4):
        at = slice(256 * i, 256 * i + 256)
        n1, inv1 = norm(tok[at, :].astype(F32))
        gn = work[at, :] * s0
        back = inv1 * (gn - n1 * jnp.mean(gn * n1, axis=-1, keepdims=True))
        o_tok[at, :] = (gr[at, :].astype(F32) + back).astype(BF)


def sum_kernel(parts, o_qkv, o_out, o_up, o_down, o_scales, *, loss_scale):
    total = parts[0].astype(F32)
    for k in range(1, 64):
        total = total + parts[k].astype(F32)
    total = total * loss_scale
    for j in range(2):
        for n in range(14):
            row = total[j * 14 + n : j * 14 + n + 1, :]
            if n < 6:
                o_qkv[j : j + 1, n * 128 : n * 128 + 128] = row
            elif n < 8:
                o_out[j : j + 1, (n - 6) * 128 : (n - 6) * 128 + 128] = row
            else:
                o_up[j : j + 1, (n - 8) * 128 : (n - 8) * 128 + 128] = row
    for j in range(6):
        for n in range(2):
            o_down[j : j + 1, n * 128 : n * 128 + 128] = total[28 + 2 * j + n : 29 + 2 * j + n, :]
    for j in range(4):
        o_scales[j // 2 : j // 2 + 1, (j % 2) * 128 : (j % 2) * 128 + 128] = total[
            40 + j : 41 + j, :
        ]


def vm(n):
    return [pl.BlockSpec(memory_space=pltpu.VMEM)] * n


def sds(shape, dtype):
    return jax.ShapeDtypeStruct(shape, dtype)


def params(mib):
    return dict(compiler_params=pltpu.CompilerParams(vmem_limit_bytes=mib * 1024 * 1024))


def swap(x, axes, odd):
    size = lax.axis_size(axes)
    pairs = [(i, i + 1) for i in range(odd, size - 1, 2)]
    return lax.ppermute(x, axes, pairs + [(b, a) for a, b in pairs])


def body(tokens, grad_out, scales, w_qkv, w_out, w_up, w_down):
    rows_total = TR * lax.axis_size(ROW)
    cols_total = TC * lax.axis_size(COL)
    core_id = lax.axis_index("core")
    half_row = lax.axis_index("zh")
    pos = jnp.stack(
        [lax.axis_index(ROW) * TR, lax.axis_index(COL) * TC, core_id, half_row]
    ).astype(jnp.int32)
    flat = TR * TC
    tok = tokens.reshape(flat, C)
    gout = grad_out.reshape(flat, C)
    smem = [pl.BlockSpec(memory_space=pltpu.SMEM)]

    even, upper = core_id == 0, half_row == 0
    head, tail = tokens[:, :3], tokens[:, TC - 3 :]
    inter = swap(jnp.where(even, head, tail), COL, 1)
    intra = swap(jnp.where(even, tail, head), COL, 0)
    before = jnp.where(even, inter, intra)
    after = jnp.where(even, intra, inter)

    def rim(lo):
        gap = jnp.zeros((7, C), BF)
        return jnp.concatenate(
            [
                tok[lo * TC : (lo + 3) * TC],
                before[lo : lo + 3].reshape(9, C),
                gap,
                after[lo : lo + 3].reshape(9, C),
                gap,
            ],
            axis=0,
        )

    top, bottom = rim(0), rim(TR - 3)
    top, bottom, w_up, w_down = lax.optimization_barrier((top, bottom, w_up, w_down))
    w_wide = jnp.concatenate([w_qkv, w_up], axis=0)
    w_tall = jnp.concatenate([w_out, w_down], axis=0)
    first = swap(jnp.where(upper, bottom, top), ROW, 0)
    second = swap(jnp.where(upper, top, bottom), ROW, 1)

    outs = pl.pallas_call(
        functools.partial(main_kernel, rows_total=rows_total, cols_total=cols_total),
        out_shape=[
            sds((flat, C), BF),
            sds((flat, C), F32),
            sds((80, C), BF),
            sds((80, C), BF),
            sds((3 * TC, C), BF),
            sds((3 * TC, C), BF),
            sds((64 * CHUNK, 128), BF),
            sds((64 * CHUNK, 128), BF),
        ],
        in_specs=smem + vm(9),
        out_specs=vm(8),
        scratch_shapes=[
            pltpu.VMEM((6, NK, 256), F32),
            pltpu.VMEM((ER, EC, 2 * C), F32),
            pltpu.VMEM((ER, EC, 2 * C), F32),
            pltpu.VMEM((TR, TC, C), F32),
            pltpu.VMEM((TR, TC, C), F32),
            pltpu.VMEM((TR, TC, C), F32),
            pltpu.VMEM((TR, TC, C), F32),
            pltpu.VMEM((NB, NK, 256), BF),
            pltpu.VMEM((flat, C), BF),
            pltpu.VMEM((flat, C), BF),
            pltpu.VMEM((flat, C), BF),
            pltpu.VMEM((flat, FF), BF),
            pltpu.VMEM((flat, FF), BF),
            pltpu.VMEM((14, 256, 128), F32),
            pltpu.VMEM((2, FF, 128), F32),
            pltpu.VMEM((2, 64 * CHUNK, 128), F32),
            pltpu.VMEM((2, 80, C), F32),
            pltpu.VMEM((2, 80, 2 * C), F32),
        ],
        name="block_backward",
        **params(44),
    )(pos, tok, gout, intra, inter, first, second, scales, w_wide, w_tall)
    gr, gh, intra, inter, first, second, keep, send = outs

    inter = swap(inter, COL, 1)
    intra = swap(intra, COL, 0)
    got = lax.ppermute(send, "core", [(0, 1), (1, 0)])
    first = swap(first, ROW, 0)
    second = swap(second, ROW, 1)
    mine = pl.pallas_call(
        add_kernel,
        out_shape=sds((64 * CHUNK, 128), BF),
        in_specs=vm(2),
        out_specs=vm(1)[0],
        name="add_core",
        **params(16),
    )(keep, got)
    parts = lax.all_to_all(mine.reshape(64, CHUNK, 128), CHIPS, 0, 0, tiled=True)
    c_first, c_second = pl.pallas_call(
        corner_kernel,
        out_shape=[sds((32, C), BF)] * 2,
        in_specs=smem + vm(2) + [pl.BlockSpec(memory_space=pl.ANY)] * 2,
        out_specs=vm(2),
        scratch_shapes=[pltpu.VMEM((2, 32, C), F32)],
        cost_estimate=pl.CostEstimate(
            flops=100 * 10**9, bytes_accessed=4 * 80 * C, transcendentals=0
        ),
        name="corners",
        **params(16),
    )(pos, intra, inter, first, second)
    c_first = swap(c_first, ROW, 0)
    c_second = swap(c_second, ROW, 1)
    grad_tokens = pl.pallas_call(
        token_kernel,
        out_shape=sds((flat, C), BF),
        in_specs=smem + vm(10),
        out_specs=vm(1)[0],
        scratch_shapes=[pltpu.VMEM((flat, C), F32)],
        cost_estimate=pl.CostEstimate(
            flops=30 * flat * C, bytes_accessed=10 * flat * C, transcendentals=0
        ),
        name="grad_tokens",
        **params(16),
    )(pos, tok, gr, gh, intra, inter, first, second, c_first, c_second, scales)
    parts, grad_tokens = lax.optimization_barrier((parts, grad_tokens))
    outs = pl.pallas_call(
        functools.partial(sum_kernel, loss_scale=1.0 / math.sqrt(rows_total * cols_total)),
        out_shape=[
            sds((2, 3 * C), F32),
            sds((2, C), F32),
            sds((2, FF), F32),
            sds((6, C), F32),
            sds((2, C), F32),
        ],
        in_specs=vm(1),
        out_specs=vm(5),
        name="weight_sums",
        **params(16),
    )(parts)
    return (grad_tokens.reshape(TR, TC, C),) + tuple(outs)


def solution(mesh):
    fine = Mesh(mesh.devices.reshape(4, 2, 4, 2, 2), ("x", "zh", "y", "zl", "core"))
    tile = P(ROW, COL, None)
    share = P(ROW + COL, None)
    return jax.shard_map(
        body,
        mesh=fine,
        in_specs=(tile, tile, P(), P(), P(), P(), P()),
        out_specs=(tile, share, share, share, share, P()),
        check_vma=False,
    )
```

```python
import functools
import math

import jax
import jax.numpy as jnp
from jax import lax
from jax.experimental import pallas as pl
from jax.experimental.pallas import tpu as pltpu
from jax.sharding import Mesh, PartitionSpec as P

HEADS = 4
C = 256
FF = 768
TR, TC = 16, 64
ER, EC = 22, 72
KR, KC = 14, 16
NK = KR * KC
NB = 16
HALO = 2 * 3 * TC + 2 * 80
CHUNK = 48
EPS = 1e-6
NEG = -1e30
BF = jnp.bfloat16
F32 = jnp.float32
GA = math.sqrt(2.0 / math.pi)
GB = GA * 0.044715

ROW = ("x", "zh")
COL = ("y", "zl", "core")
CHIPS = ("x", "zh", "y", "zl")


def nt(a, b):
    return lax.dot_general(a, b, (((1,), (1,)), ((), ())), preferred_element_type=F32)


def tn(a, b):
    return lax.dot_general(a, b, (((0,), (0,)), ((), ())), preferred_element_type=F32)


def nn(a, b):
    return jnp.dot(a, b, preferred_element_type=F32)


def norm(x):
    inverse = lax.rsqrt(jnp.mean(x * x, axis=-1, keepdims=True) + EPS)
    return x * inverse, inverse


def head_masks():
    lane = lax.broadcasted_iota(jnp.int32, (1, C), 1)
    return [(jnp.right_shift(lane, 6) == h).astype(F32) for h in range(HEADS)]


def expand(x, masks):
    return jnp.concatenate([x * m for m in masks], axis=0).astype(BF)


def pick(x, masks):
    out = x[0:64] * masks[0]
    for h in range(1, HEADS):
        out = out + x[64 * h : 64 * h + 64] * masks[h]
    return out


def main_kernel(
    pos,
    tok,
    gout,
    intra,
    inter,
    first,
    second,
    scales,
    w_wide,
    w_tall,
    o_gr,
    o_gh,
    o_side,
    o_first,
    o_second,
    o_keep,
    o_send,
    bias,
    kv,
    dkv,
    q,
    att,
    gatt,
    dq,
    probs,
    h1l,
    attb,
    h2,
    activ,
    gpre,
    gmat,
    gdown,
    pk,
    halo,
    rims,
    *,
    rows_total,
    cols_total,
):
    base_r, base_c, core, half_row = pos[0], pos[1], pos[2], pos[3]
    even = core == 0
    masks = head_masks()
    w_qkv, w_up = w_wide.at[0:C], w_wide.at[C : 2 * C]
    w_out, w_down = w_tall.at[0:C], w_tall.at[C : C + FF]

    key = lax.broadcasted_iota(jnp.int32, (NK, 1), 0)
    lane = jnp.bitwise_and(lax.broadcasted_iota(jnp.int32, (1, 256), 1), 63)
    for rb in range(2):
        k_row = base_r + rb * 8 - 3 + jnp.right_shift(key, 4)
        q_row = base_r + rb * 8 + jnp.right_shift(lane, 3)
        s_row = jnp.clip(q_row - 3, 0, rows_total - 7)
        row_ok = (k_row >= s_row) & (k_row <= s_row + 6)
        for kind, c0 in enumerate((0, 8, 56)):
            k_col = base_c + c0 - 3 + jnp.bitwise_and(key, 15)
            q_col = base_c + c0 + jnp.bitwise_and(lane, 7)
            s_col = jnp.clip(q_col - 3, 0, cols_total - 7)
            ok = row_ok & (k_col >= s_col) & (k_col <= s_col + 6)
            bias[rb * 3 + kind] = jnp.where(ok, 0.0, NEG)

    s0 = scales[0:1, :]
    s1 = scales[1:2, :]

    def hidden(x):
        return (norm(x.astype(F32))[0] * s0).astype(BF)

    kv[:, TC:, :] = jnp.zeros((ER, EC - TC, 2 * C), F32)
    for i in range(4):
        at = slice(256 * i, 256 * i + 256)
        h = hidden(tok[at, :])
        h1l[at, :] = h
        got = nn(h, w_qkv[:, :C]).astype(BF).astype(F32) * 0.125
        q[4 * i : 4 * i + 4] = got.reshape(4, TC, C)
        got = nn(h, w_qkv[:, C:])
        kv[3 + 4 * i : 7 + 4 * i, 3 : TC + 3, :] = got.reshape(4, TC, 2 * C)

    halo[...] = jnp.zeros_like(halo)
    upper = half_row == 0
    one = first[...].astype(F32)
    two = second[...].astype(F32)
    sides = ((0, jnp.where(upper, two, one)), (TR + 3, jnp.where(upper, one, two)))
    for n, (at, x) in enumerate(sides):
        halo[192 * n : 192 * n + 192, :] = x[0 : 3 * TC]
        for k in range(2):
            lo = 3 * TC + 16 * k
            halo[384 + 80 * k + 3 * at : 384 + 80 * k + 3 * at + 9, :] = x[lo : lo + 9]
    for r in range(TR):
        near = intra[r].astype(F32)
        far = inter[r].astype(F32)
        lo = 384 + 3 * r + 9
        halo[lo : lo + 3, :] = jnp.where(even, far, near)
        halo[lo + 80 : lo + 83, :] = jnp.where(even, near, far)
    h_halo = hidden(halo[...])
    got = nn(h_halo, w_qkv[:, C:])
    kv[0:3, 3 : TC + 3, :] = got[0:192].reshape(3, TC, 2 * C)
    kv[TR + 3 :, 3 : TC + 3, :] = got[192:384].reshape(3, TC, 2 * C)
    for k in range(2):
        lo = k * (TC + 3)
        for r in range(ER):
            at = 384 + 80 * k + 3 * r
            kv[r, lo : lo + 3, :] = got[at : at + 3, :]
    dkv[...] = jnp.zeros_like(dkv)

    blocks = [(rb, cb) for cb in range(8) for rb in range(2)]

    def block_of(ref, r0, c0):
        return ref[r0 : r0 + 8, c0 : c0 + 8, :].reshape(64, C)

    def slab_of(r0, c0):
        return kv[r0 : r0 + KR, c0 : c0 + KC, :].astype(BF).reshape(NK, 2 * C)

    for i, (rb, cb) in enumerate(blocks):
        r0, c0 = 8 * rb, 8 * cb
        slab = slab_of(r0, c0)
        qe = expand(block_of(q, r0, c0), masks)
        kind = 0 if cb == 0 else 2 if cb == 7 else 1
        s = nt(slab[:, :C], qe) + bias[rb * 3 + kind]
        e = jnp.exp(s - jnp.max(s, axis=0, keepdims=True))
        p = (e * (1.0 / jnp.sum(e, axis=0, keepdims=True))).astype(BF)
        probs[i] = p
        out = pick(tn(p, slab[:, C:]), masks)
        att[r0 : r0 + 8, c0 : c0 + 8, :] = out.reshape(8, 8, C)

    gsc2 = jnp.zeros((1, C), F32)
    for i in range(2):
        at = slice(512 * i, 512 * i + 512)
        a = att[8 * i : 8 * i + 8].reshape(512, C).astype(BF)
        attb[at, :] = a
        resid = (tok[at, :].astype(F32) + nn(a, w_out[...])).astype(BF).astype(F32)
        n2, inv2 = norm(resid)
        h = (n2 * s1).astype(BF)
        h2[at, :] = h
        x = nn(h, w_up[...])
        g = gout[at, :]
        ga = nt(g, w_down[...])
        xx = x * x
        t = jnp.tanh(x * (GA + GB * xx))
        half = 0.5 + 0.5 * t
        act = x * half
        activ[at, :] = act.astype(BF)
        gp = (ga * (half + act * (1.0 - t) * (GA + (3.0 * GB) * xx))).astype(BF)
        gpre[at, :] = gp
        gh = nt(gp, w_up[...])
        gn = gh * s1
        back = inv2 * (gn - n2 * jnp.mean(gn * n2, axis=-1, keepdims=True))
        gsc2 = gsc2 + jnp.sum(gh * n2, axis=0, keepdims=True)
        gr = (g.astype(F32) + back).astype(BF)
        o_gr[at, :] = gr
        gatt[8 * i : 8 * i + 8] = nt(gr, w_out[...]).astype(BF).astype(F32).reshape(8, TC, C)

    def put(first, value):
        for n in range(value.shape[1] // 128):
            gmat[first + n] = value[:, n * 128 : n * 128 + 128]

    put(6, tn(attb[...], o_gr[...]))
    put(8, tn(h2[...], gpre[...]))
    for n in range(3):
        got = tn(activ[:, n * 256 : n * 256 + 256], gout[...])
        gdown[0, n * 256 : n * 256 + 256, :] = got[:, :128]
        gdown[1, n * 256 : n * 256 + 256, :] = got[:, 128:]

    for i, (rb, cb) in enumerate(blocks):
        r0, c0 = 8 * rb, 8 * cb
        slab = slab_of(r0, c0)
        qe = expand(block_of(q, r0, c0), masks)
        ge = expand(block_of(gatt, r0, c0), masks)
        pb = probs[i]
        p = pb.astype(F32)
        gs = nt(slab[:, C:], ge)
        ds = (p * (gs - jnp.sum(p * gs, axis=0, keepdims=True))).astype(BF)
        got = pick(tn(ds, slab[:, :C]), masks) * 0.125
        dq[r0 : r0 + 8, c0 : c0 + 8, :] = got.reshape(8, 8, C)
        dkv[r0 : r0 + KR, c0 : c0 + KC, :C] += nn(ds, qe).reshape(KR, KC, C)
        dkv[r0 : r0 + KR, c0 : c0 + KC, C:] += nn(pb, ge).reshape(KR, KC, C)

    rims[0:192, :] = dkv[0:3, 3 : TC + 3, :].reshape(192, 2 * C)
    rims[192:384, :] = dkv[TR + 3 :, 3 : TC + 3, :].reshape(192, 2 * C)
    for k in range(2):
        lo = k * (TC + 3)
        for r in range(ER):
            at = 384 + 80 * k + 3 * r
            rims[at : at + 3, :] = dkv[r, lo : lo + 3, :]
        rims[384 + 80 * k + 3 * ER : 464 + 80 * k, :] = jnp.zeros((80 - 3 * ER, 2 * C), F32)
    d_rims = rims[...].astype(BF)
    g_rims = nt(d_rims, w_qkv[:, C:])
    g_left, g_right = g_rims[384:464], g_rims[464:544]
    o_side[0:48, :] = g_left[9:57]
    o_side[48:96, :] = g_right[9:57]
    work = halo
    for n, src in enumerate((g_rims[0:192], g_rims[192:384])):
        work[n * 224 : n * 224 + 192, :] = src
        for k, x in enumerate((g_left, g_right)):
            at = n * 224 + 192 + 16 * k
            work[at : at + 16, :] = x[0:16] if n == 0 else x[3 * (TR + 3) : 3 * (TR + 3) + 16]
    g_top, g_bottom = work[0:224, :], work[224:448, :]
    o_first[...] = jnp.where(upper, g_bottom, g_top).astype(BF)
    o_second[...] = jnp.where(upper, g_top, g_bottom).astype(BF)

    gq = jnp.zeros((C, C), F32)
    gkv = tn(h_halo, d_rims)
    for i in range(4):
        at = slice(256 * i, 256 * i + 256)
        d_q = dq[4 * i : 4 * i + 4].reshape(256, C).astype(BF)
        d_kv = dkv[3 + 4 * i : 7 + 4 * i, 3 : TC + 3, :].reshape(256, 2 * C).astype(BF)
        o_gh[at, :] = nt(d_q, w_qkv[:, :C]) + nt(d_kv, w_qkv[:, C:])
        h = h1l[at, :]
        gq = gq + tn(h, d_q)
        gkv = gkv + tn(h, d_kv)
    put(0, gq)
    put(2, gkv)

    prod = gq * w_qkv[:, :C].astype(F32)
    both = gkv * w_qkv[:, C:].astype(F32)
    lanes = prod[:, :128] + prod[:, 128:]
    for n in range(4):
        lanes = lanes + both[:, n * 128 : n * 128 + 128]
    gsc1 = jnp.sum(lanes.T, axis=0, keepdims=True) / s0
    rows = [gsc1[:, :128], gsc1[:, 128:], gsc2[:, :128], gsc2[:, 128:]]

    for c in range(2):
        for j in range(2):
            for n in range(14):
                pk[c, pl.ds(j * 14 + n, 64, stride=CHUNK), :] = gmat[
                    n, pl.ds(2 * c + j, 64, stride=4), :
                ]
        for j in range(6):
            for n in range(2):
                pk[c, pl.ds(28 + j * 2 + n, 64, stride=CHUNK), :] = gdown[
                    n, pl.ds(6 * c + j, 64, stride=12), :
                ]
        for j in range(4):
            pk[c, pl.ds(40 + j, 64, stride=CHUNK), :] = jnp.broadcast_to(rows[j], (64, 128))
            pk[c, pl.ds(44 + j, 64, stride=CHUNK), :] = jnp.zeros((64, 128), F32)
    o_keep[...] = pk[core].astype(BF)
    o_send[...] = pk[1 - core].astype(BF)


def add_kernel(keep, got, o_mine):
    o_mine[...] = (keep[...].astype(F32) + got[...].astype(F32)).astype(BF)


def side_kernel(pos, side, first, second, o_intra, o_inter, work):
    even, upper = pos[2] == 0, pos[3] == 0
    one = first[192:224, :].astype(F32)
    two = second[192:224, :].astype(F32)
    above, below = jnp.where(upper, two, one), jnp.where(upper, one, two)
    work[...] = side[...]
    for k in range(2):
        work[48 * k : 48 * k + 9, :] += above[16 * k : 16 * k + 9]
        work[48 * k + 39 : 48 * k + 48, :] += below[16 * k : 16 * k + 9]
    left, right = work[0:48, :], work[48:96, :]
    o_intra[...] = jnp.where(even, right, left).astype(BF)
    o_inter[...] = jnp.where(even, left, right).astype(BF)


def token_kernel(pos, tok, gr, gh, intra, inter, first, second, scales, o_tok, work):
    even, upper = pos[2] == 0, pos[3] == 0
    near = intra[...].astype(F32)
    far = inter[...].astype(F32)
    left, right = jnp.where(even, far, near), jnp.where(even, near, far)
    work[...] = gh[...]
    one = first[0 : 3 * TC, :].astype(F32)
    two = second[0 : 3 * TC, :].astype(F32)
    work[0 : 3 * TC, :] += jnp.where(upper, two, one)
    work[(TR - 3) * TC :, :] += jnp.where(upper, one, two)
    for r in range(TR):
        work[r * TC : r * TC + 3, :] += left[3 * r : 3 * r + 3]
        work[r * TC + TC - 3 : r * TC + TC, :] += right[3 * r : 3 * r + 3]
    s0 = scales[0:1, :]
    for i in range(4):
        at = slice(256 * i, 256 * i + 256)
        n1, inv1 = norm(tok[at, :].astype(F32))
        gn = work[at, :] * s0
        back = inv1 * (gn - n1 * jnp.mean(gn * n1, axis=-1, keepdims=True))
        o_tok[at, :] = (gr[at, :].astype(F32) + back).astype(BF)


def sum_kernel(parts, o_qkv, o_out, o_up, o_down, o_scales, *, loss_scale):
    total = parts[0].astype(F32)
    for k in range(1, 64):
        total = total + parts[k].astype(F32)
    total = total * loss_scale
    for j in range(2):
        for n in range(14):
            row = total[j * 14 + n : j * 14 + n + 1, :]
            if n < 6:
                o_qkv[j : j + 1, n * 128 : n * 128 + 128] = row
            elif n < 8:
                o_out[j : j + 1, (n - 6) * 128 : (n - 6) * 128 + 128] = row
            else:
                o_up[j : j + 1, (n - 8) * 128 : (n - 8) * 128 + 128] = row
    for j in range(6):
        for n in range(2):
            o_down[j : j + 1, n * 128 : n * 128 + 128] = total[28 + 2 * j + n : 29 + 2 * j + n, :]
    for j in range(4):
        o_scales[j // 2 : j // 2 + 1, (j % 2) * 128 : (j % 2) * 128 + 128] = total[
            40 + j : 41 + j, :
        ]


def vm(n):
    return [pl.BlockSpec(memory_space=pltpu.VMEM)] * n


def sds(shape, dtype):
    return jax.ShapeDtypeStruct(shape, dtype)


def params(mib):
    return dict(compiler_params=pltpu.CompilerParams(vmem_limit_bytes=mib * 1024 * 1024))


def swap(x, axes, odd):
    size = lax.axis_size(axes)
    pairs = [(i, i + 1) for i in range(odd, size - 1, 2)]
    return lax.ppermute(x, axes, pairs + [(b, a) for a, b in pairs])


def body(tokens, grad_out, scales, w_qkv, w_out, w_up, w_down):
    rows_total = TR * lax.axis_size(ROW)
    cols_total = TC * lax.axis_size(COL)
    core_id = lax.axis_index("core")
    half_row = lax.axis_index("zh")
    pos = jnp.stack(
        [lax.axis_index(ROW) * TR, lax.axis_index(COL) * TC, core_id, half_row]
    ).astype(jnp.int32)
    flat = TR * TC
    tok = tokens.reshape(flat, C)
    gout = grad_out.reshape(flat, C)
    smem = [pl.BlockSpec(memory_space=pltpu.SMEM)]

    even, upper = core_id == 0, half_row == 0
    head, tail = tokens[:, :3], tokens[:, TC - 3 :]
    inter = swap(jnp.where(even, head, tail), COL, 1)
    intra = swap(jnp.where(even, tail, head), COL, 0)
    before = jnp.where(even, inter, intra)
    after = jnp.where(even, intra, inter)

    def rim(lo):
        gap = jnp.zeros((7, C), BF)
        return jnp.concatenate(
            [
                tok[lo * TC : (lo + 3) * TC],
                before[lo : lo + 3].reshape(9, C),
                gap,
                after[lo : lo + 3].reshape(9, C),
                gap,
            ],
            axis=0,
        )

    top, bottom = rim(0), rim(TR - 3)
    top, bottom, w_up, w_down = lax.optimization_barrier((top, bottom, w_up, w_down))
    w_wide = jnp.concatenate([w_qkv, w_up], axis=0)
    w_tall = jnp.concatenate([w_out, w_down], axis=0)
    first = swap(jnp.where(upper, bottom, top), ROW, 0)
    second = swap(jnp.where(upper, top, bottom), ROW, 1)

    outs = pl.pallas_call(
        functools.partial(main_kernel, rows_total=rows_total, cols_total=cols_total),
        out_shape=[
            sds((flat, C), BF),
            sds((flat, C), F32),
            sds((96, C), F32),
            sds((224, C), BF),
            sds((224, C), BF),
            sds((64 * CHUNK, 128), BF),
            sds((64 * CHUNK, 128), BF),
        ],
        in_specs=smem + vm(9),
        out_specs=vm(7),
        scratch_shapes=[
            pltpu.VMEM((6, NK, 256), F32),
            pltpu.VMEM((ER, EC, 2 * C), F32),
            pltpu.VMEM((ER, EC, 2 * C), F32),
            pltpu.VMEM((TR, TC, C), F32),
            pltpu.VMEM((TR, TC, C), F32),
            pltpu.VMEM((TR, TC, C), F32),
            pltpu.VMEM((TR, TC, C), F32),
            pltpu.VMEM((NB, NK, 256), BF),
            pltpu.VMEM((flat, C), BF),
            pltpu.VMEM((flat, C), BF),
            pltpu.VMEM((flat, C), BF),
            pltpu.VMEM((flat, FF), BF),
            pltpu.VMEM((flat, FF), BF),
            pltpu.VMEM((14, 256, 128), F32),
            pltpu.VMEM((2, FF, 128), F32),
            pltpu.VMEM((2, 64 * CHUNK, 128), F32),
            pltpu.VMEM((HALO, C), F32),
            pltpu.VMEM((HALO, 2 * C), F32),
        ],
        name="block_backward",
        **params(44),
    )(pos, tok, gout, intra, inter, first, second, scales, w_wide, w_tall)
    gr, gh, side, first, second, keep, send = outs

    got = lax.ppermute(send, "core", [(0, 1), (1, 0)])
    first = swap(first, ROW, 0)
    second = swap(second, ROW, 1)
    mine = pl.pallas_call(
        add_kernel,
        out_shape=sds((64 * CHUNK, 128), BF),
        in_specs=vm(2),
        out_specs=vm(1)[0],
        name="add_core",
        **params(16),
    )(keep, got)
    parts = lax.all_to_all(mine.reshape(64, CHUNK, 128), CHIPS, 0, 0, tiled=True)
    intra, inter = pl.pallas_call(
        side_kernel,
        out_shape=[sds((48, C), BF)] * 2,
        in_specs=smem + vm(3),
        out_specs=vm(2),
        scratch_shapes=[pltpu.VMEM((96, C), F32)],
        cost_estimate=pl.CostEstimate(
            flops=100 * 10**9, bytes_accessed=4 * 96 * C, transcendentals=0
        ),
        name="sides",
        **params(16),
    )(pos, side, first, second)
    inter = swap(inter, COL, 1)
    intra = swap(intra, COL, 0)
    grad_tokens = pl.pallas_call(
        token_kernel,
        out_shape=sds((flat, C), BF),
        in_specs=smem + vm(8),
        out_specs=vm(1)[0],
        scratch_shapes=[pltpu.VMEM((flat, C), F32)],
        cost_estimate=pl.CostEstimate(
            flops=30 * flat * C, bytes_accessed=10 * flat * C, transcendentals=0
        ),
        name="grad_tokens",
        **params(16),
    )(pos, tok, gr, gh, intra, inter, first, second, scales)
    parts, grad_tokens = lax.optimization_barrier((parts, grad_tokens))
    outs = pl.pallas_call(
        functools.partial(sum_kernel, loss_scale=1.0 / math.sqrt(rows_total * cols_total)),
        out_shape=[
            sds((2, 3 * C), F32),
            sds((2, C), F32),
            sds((2, FF), F32),
            sds((6, C), F32),
            sds((2, C), F32),
        ],
        in_specs=vm(1),
        out_specs=vm(5),
        name="weight_sums",
        **params(16),
    )(parts)
    return (grad_tokens.reshape(TR, TC, C),) + tuple(outs)


def solution(mesh):
    fine = Mesh(mesh.devices.reshape(4, 2, 4, 2, 2), ("x", "zh", "y", "zl", "core"))
    tile = P(ROW, COL, None)
    share = P(ROW + COL, None)
    return jax.shard_map(
        body,
        mesh=fine,
        in_specs=(tile, tile, P(), P(), P(), P(), P()),
        out_specs=(tile, share, share, share, share, P()),
        check_vma=False,
    )
```

```python
import functools
import math

import jax
import jax.numpy as jnp
from jax import lax
from jax.experimental import pallas as pl
from jax.experimental.pallas import tpu as pltpu
from jax.sharding import Mesh, PartitionSpec as P

HEADS = 4
C = 256
FF = 768
TR, TC = 16, 64
ER, EC = 22, 72
KR, KC = 14, 16
NK = KR * KC
NB = 16
HALO = 2 * 3 * TC + 2 * 80
CHUNK = 48
EPS = 1e-6
NEG = -1e30
BF = jnp.bfloat16
F32 = jnp.float32
GA = math.sqrt(2.0 / math.pi)
GB = GA * 0.044715

ROW = ("x", "zh")
COL = ("y", "zl", "core")
CHIPS = ("x", "zh", "y", "zl")


def nt(a, b):
    return lax.dot_general(a, b, (((1,), (1,)), ((), ())), preferred_element_type=F32)


def tn(a, b):
    return lax.dot_general(a, b, (((0,), (0,)), ((), ())), preferred_element_type=F32)


def nn(a, b):
    return jnp.dot(a, b, preferred_element_type=F32)


def norm(x):
    inverse = lax.rsqrt(jnp.mean(x * x, axis=-1, keepdims=True) + EPS)
    return x * inverse, inverse


def first_half():
    return lax.broadcasted_iota(jnp.int32, (1, 128), 1) < 64


def expand(x, low):
    lo, hi = x[:, :128], x[:, 128:]
    none = jnp.zeros_like(lo)
    return jnp.concatenate(
        [
            jnp.concatenate([jnp.where(low, lo, 0.0), none], axis=1),
            jnp.concatenate([jnp.where(low, 0.0, lo), none], axis=1),
            jnp.concatenate([none, jnp.where(low, hi, 0.0)], axis=1),
            jnp.concatenate([none, jnp.where(low, 0.0, hi)], axis=1),
        ],
        axis=0,
    ).astype(BF)


def pick(x, low):
    lo = jnp.where(low, x[0:64, :128], x[64:128, :128])
    hi = jnp.where(low, x[128:192, 128:], x[192:256, 128:])
    return jnp.concatenate([lo, hi], axis=1)


def main_kernel(
    pos,
    tok,
    gout,
    intra,
    inter,
    first,
    second,
    scales,
    w_wide,
    w_tall,
    o_gr,
    o_gh,
    o_side,
    o_first,
    o_second,
    o_keep,
    o_send,
    bias,
    kv,
    dkv,
    q,
    att,
    gatt,
    dq,
    probs,
    h1l,
    attb,
    h2,
    activ,
    gpre,
    gmat,
    gdown,
    pk,
    halo,
    rims,
    *,
    rows_total,
    cols_total,
):
    base_r, base_c, core, half_row = pos[0], pos[1], pos[2], pos[3]
    even = core == 0
    masks = first_half()
    w_qkv, w_up = w_wide.at[0:C], w_wide.at[C : 2 * C]
    w_out, w_down = w_tall.at[0:C], w_tall.at[C : C + FF]

    key = lax.broadcasted_iota(jnp.int32, (NK, 1), 0)
    lane = jnp.bitwise_and(lax.broadcasted_iota(jnp.int32, (1, 256), 1), 63)
    for rb in range(2):
        k_row = base_r + rb * 8 - 3 + jnp.right_shift(key, 4)
        q_row = base_r + rb * 8 + jnp.right_shift(lane, 3)
        s_row = jnp.clip(q_row - 3, 0, rows_total - 7)
        row_ok = (k_row >= s_row) & (k_row <= s_row + 6)
        for kind, c0 in enumerate((0, 8, 56)):
            k_col = base_c + c0 - 3 + jnp.bitwise_and(key, 15)
            q_col = base_c + c0 + jnp.bitwise_and(lane, 7)
            s_col = jnp.clip(q_col - 3, 0, cols_total - 7)
            ok = row_ok & (k_col >= s_col) & (k_col <= s_col + 6)
            bias[rb * 3 + kind] = jnp.where(ok, 0.0, NEG)

    s0 = scales[0:1, :]
    s1 = scales[1:2, :]

    def hidden(x):
        return (norm(x.astype(F32))[0] * s0).astype(BF)

    kv[:, TC:, :] = jnp.zeros((ER, EC - TC, 2 * C), F32)
    for i in range(4):
        at = slice(256 * i, 256 * i + 256)
        h = hidden(tok[at, :])
        h1l[at, :] = h
        got = nn(h, w_qkv[:, :C]).astype(BF).astype(F32) * 0.125
        q[4 * i : 4 * i + 4] = got.reshape(4, TC, C)
        got = nn(h, w_qkv[:, C:])
        kv[3 + 4 * i : 7 + 4 * i, 3 : TC + 3, :] = got.reshape(4, TC, 2 * C)

    upper = half_row == 0
    one = first[...].astype(F32)
    two = second[...].astype(F32)
    near = intra[...].astype(F32)
    far = inter[...].astype(F32)
    halo[0:192, :] = jnp.where(upper, two, one)
    halo[192:384, :] = jnp.where(upper, one, two)
    halo[384:464, :] = jnp.where(even, far, near)
    halo[464:544, :] = jnp.where(even, near, far)
    h_halo = hidden(halo[...])
    got = nn(h_halo, w_qkv[:, C:])
    kv[0:3, 3 : TC + 3, :] = got[0:192].reshape(3, TC, 2 * C)
    kv[TR + 3 :, 3 : TC + 3, :] = got[192:384].reshape(3, TC, 2 * C)
    for k in range(2):
        lo = k * (TC + 3)
        for r in range(ER):
            at = 384 + 80 * k + 3 * r
            kv[r, lo : lo + 3, :] = got[at : at + 3, :]
    dkv[...] = jnp.zeros_like(dkv)

    blocks = [(rb, cb) for cb in range(8) for rb in range(2)]

    def block_of(ref, r0, c0):
        return ref[r0 : r0 + 8, c0 : c0 + 8, :].reshape(64, C)

    def slab_of(r0, c0):
        return kv[r0 : r0 + KR, c0 : c0 + KC, :].astype(BF).reshape(NK, 2 * C)

    for i, (rb, cb) in enumerate(blocks):
        r0, c0 = 8 * rb, 8 * cb
        slab = slab_of(r0, c0)
        qe = expand(block_of(q, r0, c0), masks)
        kind = 0 if cb == 0 else 2 if cb == 7 else 1
        s = nt(slab[:, :C], qe) + bias[rb * 3 + kind]
        e = jnp.exp(s - jnp.max(s, axis=0, keepdims=True))
        p = (e * (1.0 / jnp.sum(e, axis=0, keepdims=True))).astype(BF)
        probs[i] = p
        out = pick(tn(p, slab[:, C:]), masks)
        att[r0 : r0 + 8, c0 : c0 + 8, :] = out.reshape(8, 8, C)

    gsc2 = jnp.zeros((1, C), F32)
    for i in range(2):
        at = slice(512 * i, 512 * i + 512)
        a = att[8 * i : 8 * i + 8].reshape(512, C).astype(BF)
        attb[at, :] = a
        resid = (tok[at, :].astype(F32) + nn(a, w_out[...])).astype(BF).astype(F32)
        n2, inv2 = norm(resid)
        h = (n2 * s1).astype(BF)
        h2[at, :] = h
        x = nn(h, w_up[...])
        g = gout[at, :]
        ga = nt(g, w_down[...])
        xx = x * x
        t = jnp.tanh(x * (GA + GB * xx))
        half = 0.5 + 0.5 * t
        act = x * half
        activ[at, :] = act.astype(BF)
        gp = (ga * (half + act * (1.0 - t) * (GA + (3.0 * GB) * xx))).astype(BF)
        gpre[at, :] = gp
        gh = nt(gp, w_up[...])
        gn = gh * s1
        back = inv2 * (gn - n2 * jnp.mean(gn * n2, axis=-1, keepdims=True))
        gsc2 = gsc2 + jnp.sum(gh * n2, axis=0, keepdims=True)
        gr = (g.astype(F32) + back).astype(BF)
        o_gr[at, :] = gr
        gatt[8 * i : 8 * i + 8] = nt(gr, w_out[...]).astype(BF).astype(F32).reshape(8, TC, C)

    def put(first, value):
        for n in range(value.shape[1] // 128):
            gmat[first + n] = value[:, n * 128 : n * 128 + 128]

    put(6, tn(attb[...], o_gr[...]))
    put(8, tn(h2[...], gpre[...]))
    for n in range(3):
        got = tn(activ[:, n * 256 : n * 256 + 256], gout[...])
        gdown[0, n * 256 : n * 256 + 256, :] = got[:, :128]
        gdown[1, n * 256 : n * 256 + 256, :] = got[:, 128:]

    for i, (rb, cb) in enumerate(blocks):
        r0, c0 = 8 * rb, 8 * cb
        slab = slab_of(r0, c0)
        qe = expand(block_of(q, r0, c0), masks)
        ge = expand(block_of(gatt, r0, c0), masks)
        pb = probs[i]
        p = pb.astype(F32)
        gs = nt(slab[:, C:], ge)
        ds = (p * (gs - jnp.sum(p * gs, axis=0, keepdims=True))).astype(BF)
        got = pick(tn(ds, slab[:, :C]), masks) * 0.125
        dq[r0 : r0 + 8, c0 : c0 + 8, :] = got.reshape(8, 8, C)
        dkv[r0 : r0 + KR, c0 : c0 + KC, :C] += nn(ds, qe).reshape(KR, KC, C)
        dkv[r0 : r0 + KR, c0 : c0 + KC, C:] += nn(pb, ge).reshape(KR, KC, C)

    rims[0:192, :] = dkv[0:3, 3 : TC + 3, :].reshape(192, 2 * C)
    rims[192:384, :] = dkv[TR + 3 :, 3 : TC + 3, :].reshape(192, 2 * C)
    for k in range(2):
        lo = k * (TC + 3)
        for r in range(ER):
            at = 384 + 80 * k + 3 * r
            rims[at : at + 3, :] = dkv[r, lo : lo + 3, :]
        rims[384 + 80 * k + 3 * ER : 464 + 80 * k, :] = jnp.zeros((80 - 3 * ER, 2 * C), F32)
    d_rims = rims[...].astype(BF)
    g_rims = nt(d_rims, w_qkv[:, C:])
    g_left, g_right = g_rims[384:464], g_rims[464:544]
    o_side[0:48, :] = g_left[9:57]
    o_side[48:96, :] = g_right[9:57]
    work = halo
    for n, src in enumerate((g_rims[0:192], g_rims[192:384])):
        work[n * 224 : n * 224 + 192, :] = src
        for k, x in enumerate((g_left, g_right)):
            at = n * 224 + 192 + 16 * k
            work[at : at + 16, :] = x[0:16] if n == 0 else x[3 * (TR + 3) : 3 * (TR + 3) + 16]
    g_top, g_bottom = work[0:224, :], work[224:448, :]
    o_first[...] = jnp.where(upper, g_bottom, g_top).astype(BF)
    o_second[...] = jnp.where(upper, g_top, g_bottom).astype(BF)

    gq = jnp.zeros((C, C), F32)
    gkv = tn(h_halo, d_rims)
    for i in range(4):
        at = slice(256 * i, 256 * i + 256)
        d_q = dq[4 * i : 4 * i + 4].reshape(256, C).astype(BF)
        d_kv = dkv[3 + 4 * i : 7 + 4 * i, 3 : TC + 3, :].reshape(256, 2 * C).astype(BF)
        o_gh[at, :] = nt(d_q, w_qkv[:, :C]) + nt(d_kv, w_qkv[:, C:])
        h = h1l[at, :]
        gq = gq + tn(h, d_q)
        gkv = gkv + tn(h, d_kv)
    put(0, gq)
    put(2, gkv)

    prod = gq * w_qkv[:, :C].astype(F32)
    both = gkv * w_qkv[:, C:].astype(F32)
    lanes = prod[:, :128] + prod[:, 128:]
    for n in range(4):
        lanes = lanes + both[:, n * 128 : n * 128 + 128]
    gsc1 = jnp.sum(lanes.T, axis=0, keepdims=True) / s0
    rows = [gsc1[:, :128], gsc1[:, 128:], gsc2[:, :128], gsc2[:, 128:]]

    for c in range(2):
        for j in range(2):
            for n in range(14):
                pk[c, pl.ds(j * 14 + n, 64, stride=CHUNK), :] = gmat[
                    n, pl.ds(2 * c + j, 64, stride=4), :
                ]
        for j in range(6):
            for n in range(2):
                pk[c, pl.ds(28 + j * 2 + n, 64, stride=CHUNK), :] = gdown[
                    n, pl.ds(6 * c + j, 64, stride=12), :
                ]
        for j in range(4):
            pk[c, pl.ds(40 + j, 64, stride=CHUNK), :] = jnp.broadcast_to(rows[j], (64, 128))
            pk[c, pl.ds(44 + j, 64, stride=CHUNK), :] = jnp.zeros((64, 128), F32)
    o_keep[...] = pk[core].astype(BF)
    o_send[...] = pk[1 - core].astype(BF)


def edge_kernel(pos, tok, first, second, o_intra, o_inter, work):
    even, upper = pos[2] == 0, pos[3] == 0
    one = first[...].astype(F32)
    two = second[...].astype(F32)
    work[...] = jnp.zeros_like(work)
    for at, x in ((0, jnp.where(upper, two, one)), (TR + 3, jnp.where(upper, one, two))):
        for r in range(3):
            to = 3 * (at + r)
            work[0, to : to + 3, :] = x[r * TC : r * TC + 3]
            work[1, to : to + 3, :] = x[r * TC + TC - 3 : r * TC + TC]
    for r in range(TR):
        to = 3 * (r + 3)
        work[0, to : to + 3, :] = tok[r * TC : r * TC + 16, :].astype(F32)[0:3]
        work[1, to : to + 3, :] = tok[r * TC + TC - 16 : r * TC + TC, :].astype(F32)[13:16]
    head, tail = work[0], work[1]
    o_intra[...] = jnp.where(even, tail, head).astype(BF)
    o_inter[...] = jnp.where(even, head, tail).astype(BF)


def add_kernel(keep, got, o_mine):
    o_mine[...] = (keep[...].astype(F32) + got[...].astype(F32)).astype(BF)


def side_kernel(pos, side, first, second, o_intra, o_inter, work):
    even, upper = pos[2] == 0, pos[3] == 0
    one = first[192:224, :].astype(F32)
    two = second[192:224, :].astype(F32)
    above, below = jnp.where(upper, two, one), jnp.where(upper, one, two)
    work[...] = side[...]
    for k in range(2):
        work[48 * k : 48 * k + 9, :] += above[16 * k : 16 * k + 9]
        work[48 * k + 39 : 48 * k + 48, :] += below[16 * k : 16 * k + 9]
    left, right = work[0:48, :], work[48:96, :]
    o_intra[...] = jnp.where(even, right, left).astype(BF)
    o_inter[...] = jnp.where(even, left, right).astype(BF)


def token_kernel(pos, tok, gr, gh, intra, inter, first, second, scales, o_tok, work):
    even, upper = pos[2] == 0, pos[3] == 0
    near = intra[...].astype(F32)
    far = inter[...].astype(F32)
    left, right = jnp.where(even, far, near), jnp.where(even, near, far)
    work[...] = gh[...]
    one = first[0 : 3 * TC, :].astype(F32)
    two = second[0 : 3 * TC, :].astype(F32)
    work[0 : 3 * TC, :] += jnp.where(upper, two, one)
    work[(TR - 3) * TC :, :] += jnp.where(upper, one, two)
    for r in range(TR):
        work[r * TC : r * TC + 3, :] += left[3 * r : 3 * r + 3]
        work[r * TC + TC - 3 : r * TC + TC, :] += right[3 * r : 3 * r + 3]
    s0 = scales[0:1, :]
    for i in range(4):
        at = slice(256 * i, 256 * i + 256)
        n1, inv1 = norm(tok[at, :].astype(F32))
        gn = work[at, :] * s0
        back = inv1 * (gn - n1 * jnp.mean(gn * n1, axis=-1, keepdims=True))
        o_tok[at, :] = (gr[at, :].astype(F32) + back).astype(BF)


def sum_kernel(parts, o_qkv, o_out, o_up, o_down, o_scales, *, loss_scale):
    total = parts[0].astype(F32)
    for k in range(1, 64):
        total = total + parts[k].astype(F32)
    total = total * loss_scale
    for j in range(2):
        for n in range(14):
            row = total[j * 14 + n : j * 14 + n + 1, :]
            if n < 6:
                o_qkv[j : j + 1, n * 128 : n * 128 + 128] = row
            elif n < 8:
                o_out[j : j + 1, (n - 6) * 128 : (n - 6) * 128 + 128] = row
            else:
                o_up[j : j + 1, (n - 8) * 128 : (n - 8) * 128 + 128] = row
    for j in range(6):
        for n in range(2):
            o_down[j : j + 1, n * 128 : n * 128 + 128] = total[28 + 2 * j + n : 29 + 2 * j + n, :]
    for j in range(4):
        o_scales[j // 2 : j // 2 + 1, (j % 2) * 128 : (j % 2) * 128 + 128] = total[
            40 + j : 41 + j, :
        ]


def vm(n):
    return [pl.BlockSpec(memory_space=pltpu.VMEM)] * n


def sds(shape, dtype):
    return jax.ShapeDtypeStruct(shape, dtype)


def params(mib):
    return dict(compiler_params=pltpu.CompilerParams(vmem_limit_bytes=mib * 1024 * 1024))


def swap(x, axes, odd):
    size = lax.axis_size(axes)
    pairs = [(i, i + 1) for i in range(odd, size - 1, 2)]
    return lax.ppermute(x, axes, pairs + [(b, a) for a, b in pairs])


def body(tokens, grad_out, scales, w_qkv, w_out, w_up, w_down):
    rows_total = TR * lax.axis_size(ROW)
    cols_total = TC * lax.axis_size(COL)
    core_id = lax.axis_index("core")
    half_row = lax.axis_index("zh")
    pos = jnp.stack(
        [lax.axis_index(ROW) * TR, lax.axis_index(COL) * TC, core_id, half_row]
    ).astype(jnp.int32)
    flat = TR * TC
    tok = tokens.reshape(flat, C)
    gout = grad_out.reshape(flat, C)
    smem = [pl.BlockSpec(memory_space=pltpu.SMEM)]

    upper = half_row == 0
    top, bottom = tok[: 3 * TC], tok[(TR - 3) * TC :]
    first, second = jnp.where(upper, bottom, top), jnp.where(upper, top, bottom)
    first, second, w_up, w_down = lax.optimization_barrier((first, second, w_up, w_down))
    w_wide = jnp.concatenate([w_qkv, w_up], axis=0)
    w_tall = jnp.concatenate([w_out, w_down], axis=0)
    first = swap(first, ROW, 0)
    second = swap(second, ROW, 1)
    intra, inter = pl.pallas_call(
        edge_kernel,
        out_shape=[sds((80, C), BF)] * 2,
        in_specs=smem + vm(3),
        out_specs=vm(2),
        scratch_shapes=[pltpu.VMEM((2, 80, C), F32)],
        name="edges",
        **params(16),
    )(pos, tok, first, second)
    inter = swap(inter, COL, 1)
    intra = swap(intra, COL, 0)

    outs = pl.pallas_call(
        functools.partial(main_kernel, rows_total=rows_total, cols_total=cols_total),
        out_shape=[
            sds((flat, C), BF),
            sds((flat, C), F32),
            sds((96, C), F32),
            sds((224, C), BF),
            sds((224, C), BF),
            sds((64 * CHUNK, 128), BF),
            sds((64 * CHUNK, 128), BF),
        ],
        in_specs=smem + vm(9),
        out_specs=vm(7),
        scratch_shapes=[
            pltpu.VMEM((6, NK, 256), F32),
            pltpu.VMEM((ER, EC, 2 * C), F32),
            pltpu.VMEM((ER, EC, 2 * C), F32),
            pltpu.VMEM((TR, TC, C), F32),
            pltpu.VMEM((TR, TC, C), F32),
            pltpu.VMEM((TR, TC, C), F32),
            pltpu.VMEM((TR, TC, C), F32),
            pltpu.VMEM((NB, NK, 256), BF),
            pltpu.VMEM((flat, C), BF),
            pltpu.VMEM((flat, C), BF),
            pltpu.VMEM((flat, C), BF),
            pltpu.VMEM((flat, FF), BF),
            pltpu.VMEM((flat, FF), BF),
            pltpu.VMEM((14, 256, 128), F32),
            pltpu.VMEM((2, FF, 128), F32),
            pltpu.VMEM((2, 64 * CHUNK, 128), F32),
            pltpu.VMEM((HALO, C), F32),
            pltpu.VMEM((HALO, 2 * C), F32),
        ],
        name="block_backward",
        **params(44),
    )(pos, tok, gout, intra, inter, first, second, scales, w_wide, w_tall)
    gr, gh, side, first, second, keep, send = outs

    got = lax.ppermute(send, "core", [(0, 1), (1, 0)])
    first = swap(first, ROW, 0)
    second = swap(second, ROW, 1)
    mine = pl.pallas_call(
        add_kernel,
        out_shape=sds((64 * CHUNK, 128), BF),
        in_specs=vm(2),
        out_specs=vm(1)[0],
        name="add_core",
        **params(16),
    )(keep, got)
    parts = lax.all_to_all(mine.reshape(64, CHUNK, 128), CHIPS, 0, 0, tiled=True)
    intra, inter = pl.pallas_call(
        side_kernel,
        out_shape=[sds((48, C), BF)] * 2,
        in_specs=smem + vm(3),
        out_specs=vm(2),
        scratch_shapes=[pltpu.VMEM((96, C), F32)],
        cost_estimate=pl.CostEstimate(
            flops=100 * 10**9, bytes_accessed=4 * 96 * C, transcendentals=0
        ),
        name="sides",
        **params(16),
    )(pos, side, first, second)
    inter = swap(inter, COL, 1)
    intra = swap(intra, COL, 0)
    grad_tokens = pl.pallas_call(
        token_kernel,
        out_shape=sds((flat, C), BF),
        in_specs=smem + vm(8),
        out_specs=vm(1)[0],
        scratch_shapes=[pltpu.VMEM((flat, C), F32)],
        cost_estimate=pl.CostEstimate(
            flops=30 * flat * C, bytes_accessed=10 * flat * C, transcendentals=0
        ),
        name="grad_tokens",
        **params(16),
    )(pos, tok, gr, gh, intra, inter, first, second, scales)
    parts, grad_tokens = lax.optimization_barrier((parts, grad_tokens))
    outs = pl.pallas_call(
        functools.partial(sum_kernel, loss_scale=1.0 / math.sqrt(rows_total * cols_total)),
        out_shape=[
            sds((2, 3 * C), F32),
            sds((2, C), F32),
            sds((2, FF), F32),
            sds((6, C), F32),
            sds((2, C), F32),
        ],
        in_specs=vm(1),
        out_specs=vm(5),
        name="weight_sums",
        **params(16),
    )(parts)
    return (grad_tokens.reshape(TR, TC, C),) + tuple(outs)


def solution(mesh):
    fine = Mesh(mesh.devices.reshape(4, 2, 4, 2, 2), ("x", "zh", "y", "zl", "core"))
    tile = P(ROW, COL, None)
    share = P(ROW + COL, None)
    return jax.shard_map(
        body,
        mesh=fine,
        in_specs=(tile, tile, P(), P(), P(), P(), P()),
        out_specs=(tile, share, share, share, share, P()),
        check_vma=False,
    )
```

```python
import functools
import math

import jax
import jax.numpy as jnp
from jax import lax
from jax.experimental import pallas as pl
from jax.experimental.pallas import tpu as pltpu
from jax.sharding import Mesh, PartitionSpec as P

HEADS = 4
C = 256
FF = 768
TR, TC = 16, 64
ER, EC = 22, 72
KR, KC = 14, 16
NK = KR * KC
NB = 16
HALO = 2 * 3 * TC + 2 * 80
CHUNK = 48
EPS = 1e-6
NEG = -1e30
BF = jnp.bfloat16
F32 = jnp.float32
GA = math.sqrt(2.0 / math.pi)
GB = GA * 0.044715

ROW = ("x", "zh")
COL = ("y", "zl", "core")
CHIPS = ("x", "zh", "y", "zl")


def nt(a, b):
    return lax.dot_general(a, b, (((1,), (1,)), ((), ())), preferred_element_type=F32)


def tn(a, b):
    return lax.dot_general(a, b, (((0,), (0,)), ((), ())), preferred_element_type=F32)


def nn(a, b):
    return jnp.dot(a, b, preferred_element_type=F32)


def norm(x):
    inverse = lax.rsqrt(jnp.mean(x * x, axis=-1, keepdims=True) + EPS)
    return x * inverse, inverse


def first_half():
    return lax.broadcasted_iota(jnp.int32, (1, 128), 1) < 64


def expand(x, low):
    lo, hi = x[:, :128], x[:, 128:]
    none = jnp.zeros_like(lo)
    return jnp.concatenate(
        [
            jnp.concatenate([jnp.where(low, lo, 0.0), none], axis=1),
            jnp.concatenate([jnp.where(low, 0.0, lo), none], axis=1),
            jnp.concatenate([none, jnp.where(low, hi, 0.0)], axis=1),
            jnp.concatenate([none, jnp.where(low, 0.0, hi)], axis=1),
        ],
        axis=0,
    ).astype(BF)


def pick(x, low):
    lo = jnp.where(low, x[0:64, :128], x[64:128, :128])
    hi = jnp.where(low, x[128:192, 128:], x[192:256, 128:])
    return jnp.concatenate([lo, hi], axis=1)


def main_kernel(
    pos,
    tok,
    gout,
    intra,
    inter,
    first,
    second,
    scales,
    w_wide,
    w_tall,
    o_gr,
    o_gh,
    o_side,
    o_first,
    o_second,
    o_keep,
    o_send,
    bias,
    kv,
    dkv,
    q,
    att,
    gatt,
    dq,
    probs,
    h1l,
    attb,
    h2,
    activ,
    gpre,
    gmat,
    gdown,
    pk,
    halo,
    rims,
    *,
    rows_total,
    cols_total,
):
    base_r, base_c, core, half_row = pos[0], pos[1], pos[2], pos[3]
    even = core == 0
    masks = first_half()
    w_qkv, w_up = w_wide.at[0:C], w_wide.at[C : 2 * C]
    w_out, w_down = w_tall.at[0:C], w_tall.at[C : C + FF]

    key = lax.broadcasted_iota(jnp.int32, (NK, 1), 0)
    lane = jnp.bitwise_and(lax.broadcasted_iota(jnp.int32, (1, 256), 1), 63)
    for rb in range(2):
        k_row = base_r + rb * 8 - 3 + jnp.right_shift(key, 4)
        q_row = base_r + rb * 8 + jnp.right_shift(lane, 3)
        s_row = jnp.clip(q_row - 3, 0, rows_total - 7)
        row_ok = (k_row >= s_row) & (k_row <= s_row + 6)
        for kind, c0 in enumerate((0, 8, 56)):
            k_col = base_c + c0 - 3 + jnp.bitwise_and(key, 15)
            q_col = base_c + c0 + jnp.bitwise_and(lane, 7)
            s_col = jnp.clip(q_col - 3, 0, cols_total - 7)
            ok = row_ok & (k_col >= s_col) & (k_col <= s_col + 6)
            bias[rb * 3 + kind] = jnp.where(ok, 0.0, NEG)

    s0 = scales[0:1, :]
    s1 = scales[1:2, :]

    def hidden(x):
        return (norm(x.astype(F32))[0] * s0).astype(BF)

    kv[:, TC:, :] = jnp.zeros((ER, EC - TC, 2 * C), F32)
    for i in range(4):
        at = slice(256 * i, 256 * i + 256)
        h = hidden(tok[at, :])
        h1l[at, :] = h
        got = nn(h, w_qkv[:, :C]).astype(BF).astype(F32) * 0.125
        q[4 * i : 4 * i + 4] = got.reshape(4, TC, C)
        got = nn(h, w_qkv[:, C:])
        kv[3 + 4 * i : 7 + 4 * i, 3 : TC + 3, :] = got.reshape(4, TC, 2 * C)

    upper = half_row == 0
    one = first[...].astype(F32)
    two = second[...].astype(F32)
    near = intra[...].astype(F32)
    far = inter[...].astype(F32)
    halo[0:192, :] = jnp.where(upper, two, one)
    halo[192:384, :] = jnp.where(upper, one, two)
    halo[384:464, :] = jnp.where(even, far, near)
    halo[464:544, :] = jnp.where(even, near, far)
    h_halo = hidden(halo[...])
    got = nn(h_halo, w_qkv[:, C:])
    kv[0:3, 3 : TC + 3, :] = got[0:192].reshape(3, TC, 2 * C)
    kv[TR + 3 :, 3 : TC + 3, :] = got[192:384].reshape(3, TC, 2 * C)
    for k in range(2):
        lo = k * (TC + 3)
        for r in range(ER):
            at = 384 + 80 * k + 3 * r
            kv[r, lo : lo + 3, :] = got[at : at + 3, :]
    dkv[...] = jnp.zeros_like(dkv)

    blocks = [(rb, cb) for odd in range(2) for rb in range(2) for cb in range(odd, 8, 2)]

    def block_of(ref, r0, c0):
        return ref[r0 : r0 + 8, c0 : c0 + 8, :].reshape(64, C)

    def slab_of(r0, c0):
        return kv[r0 : r0 + KR, c0 : c0 + KC, :].astype(BF).reshape(NK, 2 * C)

    for i, (rb, cb) in enumerate(blocks):
        r0, c0 = 8 * rb, 8 * cb
        slab = slab_of(r0, c0)
        qe = expand(block_of(q, r0, c0), masks)
        kind = 0 if cb == 0 else 2 if cb == 7 else 1
        s = nt(slab[:, :C], qe) + bias[rb * 3 + kind]
        e = jnp.exp(s - jnp.max(s, axis=0, keepdims=True))
        p = (e * (1.0 / jnp.sum(e, axis=0, keepdims=True))).astype(BF)
        probs[i] = p
        out = pick(tn(p, slab[:, C:]), masks)
        att[r0 : r0 + 8, c0 : c0 + 8, :] = out.reshape(8, 8, C)

    gsc2 = jnp.zeros((1, C), F32)
    for i in range(2):
        at = slice(512 * i, 512 * i + 512)
        a = att[8 * i : 8 * i + 8].reshape(512, C).astype(BF)
        attb[at, :] = a
        resid = (tok[at, :].astype(F32) + nn(a, w_out[...])).astype(BF).astype(F32)
        n2, inv2 = norm(resid)
        h = (n2 * s1).astype(BF)
        h2[at, :] = h
        x = nn(h, w_up[...])
        g = gout[at, :]
        ga = nt(g, w_down[...])
        xx = x * x
        t = jnp.tanh(x * (GA + GB * xx))
        half = 0.5 + 0.5 * t
        act = x * half
        activ[at, :] = act.astype(BF)
        gp = (ga * (half + act * (1.0 - t) * (GA + (3.0 * GB) * xx))).astype(BF)
        gpre[at, :] = gp
        gh = nt(gp, w_up[...])
        gn = gh * s1
        back = inv2 * (gn - n2 * jnp.mean(gn * n2, axis=-1, keepdims=True))
        gsc2 = gsc2 + jnp.sum(gh * n2, axis=0, keepdims=True)
        gr = (g.astype(F32) + back).astype(BF)
        o_gr[at, :] = gr
        gatt[8 * i : 8 * i + 8] = nt(gr, w_out[...]).astype(BF).astype(F32).reshape(8, TC, C)

    def put(first, value):
        for n in range(value.shape[1] // 128):
            gmat[first + n] = value[:, n * 128 : n * 128 + 128]

    put(6, tn(attb[...], o_gr[...]))
    put(8, tn(h2[...], gpre[...]))
    for n in range(3):
        got = tn(activ[:, n * 256 : n * 256 + 256], gout[...])
        gdown[0, n * 256 : n * 256 + 256, :] = got[:, :128]
        gdown[1, n * 256 : n * 256 + 256, :] = got[:, 128:]

    def pack(c, j, n):
        pk[c, pl.ds(j * 14 + n, 64, stride=CHUNK), :] = gmat[n, pl.ds(2 * c + j, 64, stride=4), :]

    def pack_down(c, j, n):
        pk[c, pl.ds(28 + j * 2 + n, 64, stride=CHUNK), :] = gdown[
            n, pl.ds(6 * c + j, 64, stride=12), :
        ]

    for c in range(2):
        for j in range(2):
            for n in range(6, 14):
                pack(c, j, n)
        for j in range(6):
            for n in range(2):
                pack_down(c, j, n)

    for i, (rb, cb) in enumerate(blocks):
        r0, c0 = 8 * rb, 8 * cb
        slab = slab_of(r0, c0)
        qe = expand(block_of(q, r0, c0), masks)
        ge = expand(block_of(gatt, r0, c0), masks)
        pb = probs[i]
        p = pb.astype(F32)
        gs = nt(slab[:, C:], ge)
        ds = (p * (gs - jnp.sum(p * gs, axis=0, keepdims=True))).astype(BF)
        got = pick(tn(ds, slab[:, :C]), masks) * 0.125
        dq[r0 : r0 + 8, c0 : c0 + 8, :] = got.reshape(8, 8, C)
        dkv[r0 : r0 + KR, c0 : c0 + KC, :C] += nn(ds, qe).reshape(KR, KC, C)
        dkv[r0 : r0 + KR, c0 : c0 + KC, C:] += nn(pb, ge).reshape(KR, KC, C)

    rims[0:192, :] = dkv[0:3, 3 : TC + 3, :].reshape(192, 2 * C)
    rims[192:384, :] = dkv[TR + 3 :, 3 : TC + 3, :].reshape(192, 2 * C)
    for k in range(2):
        lo = k * (TC + 3)
        for r in range(ER):
            at = 384 + 80 * k + 3 * r
            rims[at : at + 3, :] = dkv[r, lo : lo + 3, :]
        rims[384 + 80 * k + 3 * ER : 464 + 80 * k, :] = jnp.zeros((80 - 3 * ER, 2 * C), F32)
    d_rims = rims[...].astype(BF)
    g_rims = nt(d_rims, w_qkv[:, C:])
    g_left, g_right = g_rims[384:464], g_rims[464:544]
    o_side[0:48, :] = g_left[9:57]
    o_side[48:96, :] = g_right[9:57]
    work = halo
    for n, src in enumerate((g_rims[0:192], g_rims[192:384])):
        work[n * 224 : n * 224 + 192, :] = src
        for k, x in enumerate((g_left, g_right)):
            at = n * 224 + 192 + 16 * k
            work[at : at + 16, :] = x[0:16] if n == 0 else x[3 * (TR + 3) : 3 * (TR + 3) + 16]
    g_top, g_bottom = work[0:224, :], work[224:448, :]
    o_first[...] = jnp.where(upper, g_bottom, g_top).astype(BF)
    o_second[...] = jnp.where(upper, g_top, g_bottom).astype(BF)

    gq = jnp.zeros((C, C), F32)
    gkv = tn(h_halo, d_rims)
    for i in range(2):
        at = slice(512 * i, 512 * i + 512)
        d_q = dq[8 * i : 8 * i + 8].reshape(512, C).astype(BF)
        d_kv = dkv[3 + 8 * i : 11 + 8 * i, 3 : TC + 3, :].reshape(512, 2 * C).astype(BF)
        o_gh[at, :] = nt(d_q, w_qkv[:, :C]) + nt(d_kv, w_qkv[:, C:])
        h = h1l[at, :]
        gq = gq + tn(h, d_q)
        gkv = gkv + tn(h, d_kv)
    put(0, gq)
    put(2, gkv)

    prod = gq * w_qkv[:, :C].astype(F32)
    both = gkv * w_qkv[:, C:].astype(F32)
    lanes = prod[:, :128] + prod[:, 128:]
    for n in range(4):
        lanes = lanes + both[:, n * 128 : n * 128 + 128]
    gsc1 = jnp.sum(lanes.T, axis=0, keepdims=True) / s0
    rows = [gsc1[:, :128], gsc1[:, 128:], gsc2[:, :128], gsc2[:, 128:]]

    for c in range(2):
        for j in range(2):
            for n in range(6):
                pack(c, j, n)
        for j in range(4):
            pk[c, pl.ds(40 + j, 64, stride=CHUNK), :] = jnp.broadcast_to(rows[j], (64, 128))
            pk[c, pl.ds(44 + j, 64, stride=CHUNK), :] = jnp.zeros((64, 128), F32)
    o_keep[...] = pk[core].astype(BF)
    o_send[...] = pk[1 - core].astype(BF)


def edge_kernel(pos, tok, first, second, o_intra, o_inter, work):
    even, upper = pos[2] == 0, pos[3] == 0
    one = first[...].astype(F32)
    two = second[...].astype(F32)
    work[...] = jnp.zeros_like(work)
    for at, x in ((0, jnp.where(upper, two, one)), (TR + 3, jnp.where(upper, one, two))):
        for r in range(3):
            to = 3 * (at + r)
            work[0, to : to + 3, :] = x[r * TC : r * TC + 3]
            work[1, to : to + 3, :] = x[r * TC + TC - 3 : r * TC + TC]
    for r in range(TR):
        to = 3 * (r + 3)
        work[0, to : to + 3, :] = tok[r * TC : r * TC + 16, :].astype(F32)[0:3]
        work[1, to : to + 3, :] = tok[r * TC + TC - 16 : r * TC + TC, :].astype(F32)[13:16]
    head, tail = work[0], work[1]
    o_intra[...] = jnp.where(even, tail, head).astype(BF)
    o_inter[...] = jnp.where(even, head, tail).astype(BF)


def add_kernel(keep, got, o_mine):
    o_mine[...] = (keep[...].astype(F32) + got[...].astype(F32)).astype(BF)


def side_kernel(pos, side, first, second, o_intra, o_inter, work):
    even, upper = pos[2] == 0, pos[3] == 0
    one = first[192:224, :].astype(F32)
    two = second[192:224, :].astype(F32)
    above, below = jnp.where(upper, two, one), jnp.where(upper, one, two)
    work[...] = side[...]
    for k in range(2):
        work[48 * k : 48 * k + 9, :] += above[16 * k : 16 * k + 9]
        work[48 * k + 39 : 48 * k + 48, :] += below[16 * k : 16 * k + 9]
    left, right = work[0:48, :], work[48:96, :]
    o_intra[...] = jnp.where(even, right, left).astype(BF)
    o_inter[...] = jnp.where(even, left, right).astype(BF)


def token_kernel(pos, tok, gr, gh, intra, inter, first, second, scales, o_tok, work):
    even, upper = pos[2] == 0, pos[3] == 0
    near = intra[...].astype(F32)
    far = inter[...].astype(F32)
    left, right = jnp.where(even, far, near), jnp.where(even, near, far)
    work[...] = gh[...]
    one = first[0 : 3 * TC, :].astype(F32)
    two = second[0 : 3 * TC, :].astype(F32)
    work[0 : 3 * TC, :] += jnp.where(upper, two, one)
    work[(TR - 3) * TC :, :] += jnp.where(upper, one, two)
    for r in range(TR):
        work[r * TC : r * TC + 3, :] += left[3 * r : 3 * r + 3]
        work[r * TC + TC - 3 : r * TC + TC, :] += right[3 * r : 3 * r + 3]
    s0 = scales[0:1, :]
    for i in range(4):
        at = slice(256 * i, 256 * i + 256)
        n1, inv1 = norm(tok[at, :].astype(F32))
        gn = work[at, :] * s0
        back = inv1 * (gn - n1 * jnp.mean(gn * n1, axis=-1, keepdims=True))
        o_tok[at, :] = (gr[at, :].astype(F32) + back).astype(BF)


def sum_kernel(parts, o_qkv, o_out, o_up, o_down, o_scales, *, loss_scale):
    total = parts[0].astype(F32)
    for k in range(1, 64):
        total = total + parts[k].astype(F32)
    total = total * loss_scale
    for j in range(2):
        for n in range(14):
            row = total[j * 14 + n : j * 14 + n + 1, :]
            if n < 6:
                o_qkv[j : j + 1, n * 128 : n * 128 + 128] = row
            elif n < 8:
                o_out[j : j + 1, (n - 6) * 128 : (n - 6) * 128 + 128] = row
            else:
                o_up[j : j + 1, (n - 8) * 128 : (n - 8) * 128 + 128] = row
    for j in range(6):
        for n in range(2):
            o_down[j : j + 1, n * 128 : n * 128 + 128] = total[28 + 2 * j + n : 29 + 2 * j + n, :]
    for j in range(4):
        o_scales[j // 2 : j // 2 + 1, (j % 2) * 128 : (j % 2) * 128 + 128] = total[
            40 + j : 41 + j, :
        ]


def vm(n):
    return [pl.BlockSpec(memory_space=pltpu.VMEM)] * n


def sds(shape, dtype):
    return jax.ShapeDtypeStruct(shape, dtype)


def params(mib):
    return dict(compiler_params=pltpu.CompilerParams(vmem_limit_bytes=mib * 1024 * 1024))


def swap(x, axes, odd):
    size = lax.axis_size(axes)
    pairs = [(i, i + 1) for i in range(odd, size - 1, 2)]
    return lax.ppermute(x, axes, pairs + [(b, a) for a, b in pairs])


def body(tokens, grad_out, scales, w_qkv, w_out, w_up, w_down):
    rows_total = TR * lax.axis_size(ROW)
    cols_total = TC * lax.axis_size(COL)
    core_id = lax.axis_index("core")
    half_row = lax.axis_index("zh")
    pos = jnp.stack(
        [lax.axis_index(ROW) * TR, lax.axis_index(COL) * TC, core_id, half_row]
    ).astype(jnp.int32)
    flat = TR * TC
    tok = tokens.reshape(flat, C)
    gout = grad_out.reshape(flat, C)
    smem = [pl.BlockSpec(memory_space=pltpu.SMEM)]

    upper = half_row == 0
    top, bottom = tok[: 3 * TC], tok[(TR - 3) * TC :]
    first, second = jnp.where(upper, bottom, top), jnp.where(upper, top, bottom)
    first, second, w_up, w_down = lax.optimization_barrier((first, second, w_up, w_down))
    w_wide = jnp.concatenate([w_qkv, w_up], axis=0)
    w_tall = jnp.concatenate([w_out, w_down], axis=0)
    first = swap(first, ROW, 0)
    second = swap(second, ROW, 1)
    intra, inter = pl.pallas_call(
        edge_kernel,
        out_shape=[sds((80, C), BF)] * 2,
        in_specs=smem + vm(3),
        out_specs=vm(2),
        scratch_shapes=[pltpu.VMEM((2, 80, C), F32)],
        name="edges",
        **params(16),
    )(pos, tok, first, second)
    inter = swap(inter, COL, 1)
    intra = swap(intra, COL, 0)

    outs = pl.pallas_call(
        functools.partial(main_kernel, rows_total=rows_total, cols_total=cols_total),
        out_shape=[
            sds((flat, C), BF),
            sds((flat, C), F32),
            sds((96, C), F32),
            sds((224, C), BF),
            sds((224, C), BF),
            sds((64 * CHUNK, 128), BF),
            sds((64 * CHUNK, 128), BF),
        ],
        in_specs=smem + vm(9),
        out_specs=vm(7),
        scratch_shapes=[
            pltpu.VMEM((6, NK, 256), F32),
            pltpu.VMEM((ER, EC, 2 * C), F32),
            pltpu.VMEM((ER, EC, 2 * C), F32),
            pltpu.VMEM((TR, TC, C), F32),
            pltpu.VMEM((TR, TC, C), F32),
            pltpu.VMEM((TR, TC, C), F32),
            pltpu.VMEM((TR, TC, C), F32),
            pltpu.VMEM((NB, NK, 256), BF),
            pltpu.VMEM((flat, C), BF),
            pltpu.VMEM((flat, C), BF),
            pltpu.VMEM((flat, C), BF),
            pltpu.VMEM((flat, FF), BF),
            pltpu.VMEM((flat, FF), BF),
            pltpu.VMEM((14, 256, 128), F32),
            pltpu.VMEM((2, FF, 128), F32),
            pltpu.VMEM((2, 64 * CHUNK, 128), F32),
            pltpu.VMEM((HALO, C), F32),
            pltpu.VMEM((HALO, 2 * C), F32),
        ],
        name="block_backward",
        **params(44),
    )(pos, tok, gout, intra, inter, first, second, scales, w_wide, w_tall)
    gr, gh, side, first, second, keep, send = outs

    got = lax.ppermute(send, "core", [(0, 1), (1, 0)])
    first = swap(first, ROW, 0)
    second = swap(second, ROW, 1)
    mine = pl.pallas_call(
        add_kernel,
        out_shape=sds((64 * CHUNK, 128), BF),
        in_specs=vm(2),
        out_specs=vm(1)[0],
        name="add_core",
        **params(16),
    )(keep, got)
    parts = lax.all_to_all(mine.reshape(64, CHUNK, 128), CHIPS, 0, 0, tiled=True)
    intra, inter = pl.pallas_call(
        side_kernel,
        out_shape=[sds((48, C), BF)] * 2,
        in_specs=smem + vm(3),
        out_specs=vm(2),
        scratch_shapes=[pltpu.VMEM((96, C), F32)],
        cost_estimate=pl.CostEstimate(
            flops=100 * 10**9, bytes_accessed=4 * 96 * C, transcendentals=0
        ),
        name="sides",
        **params(16),
    )(pos, side, first, second)
    inter = swap(inter, COL, 1)
    intra = swap(intra, COL, 0)
    grad_tokens = pl.pallas_call(
        token_kernel,
        out_shape=sds((flat, C), BF),
        in_specs=smem + vm(8),
        out_specs=vm(1)[0],
        scratch_shapes=[pltpu.VMEM((flat, C), F32)],
        cost_estimate=pl.CostEstimate(
            flops=30 * flat * C, bytes_accessed=10 * flat * C, transcendentals=0
        ),
        name="grad_tokens",
        **params(16),
    )(pos, tok, gr, gh, intra, inter, first, second, scales)
    parts, grad_tokens = lax.optimization_barrier((parts, grad_tokens))
    outs = pl.pallas_call(
        functools.partial(sum_kernel, loss_scale=1.0 / math.sqrt(rows_total * cols_total)),
        out_shape=[
            sds((2, 3 * C), F32),
            sds((2, C), F32),
            sds((2, FF), F32),
            sds((6, C), F32),
            sds((2, C), F32),
        ],
        in_specs=vm(1),
        out_specs=vm(5),
        name="weight_sums",
        **params(16),
    )(parts)
    return (grad_tokens.reshape(TR, TC, C),) + tuple(outs)


def solution(mesh):
    fine = Mesh(mesh.devices.reshape(4, 2, 4, 2, 2), ("x", "zh", "y", "zl", "core"))
    tile = P(ROW, COL, None)
    share = P(ROW + COL, None)
    return jax.shard_map(
        body,
        mesh=fine,
        in_specs=(tile, tile, P(), P(), P(), P(), P()),
        out_specs=(tile, share, share, share, share, P()),
        check_vma=False,
    )
```
